32 devices in a mesh: tm: 16 (over z, y, x), dp: 2 (over core).
Axes of the slice: x: 2, y: 2, z: 4, core: 2. Of those that a mesh axis runs over, the one named last changes fastest.
Arguments:
- frame_tokens: bfloat16 [2, 48, 64, 1280], P('dp', 'tm'), may hold values from -8 to 8
- visible: int32 [2, 48, 64], P('dp'), may hold values from 0 to 2
- grad_output: bfloat16 [2, 48, 64, 1280], P('dp', 'tm'), may hold values from -6 to 6
- norm_gain: float32 [1280], replicated, may hold values from 0.1 to 1.9
- query_weight: bfloat16 [1280, 640], P('tm'), may hold values from -1.5 to 1.5
- key_weight: bfloat16 [1280, 640], P('tm'), may hold values from -1.5 to 1.5
- value_weight: bfloat16 [1280, 640], P('tm'), may hold values from -0.15625 to 0.15625
- output_weight: bfloat16 [640, 1280], P('tm'), may hold values from -0.25 to 0.25
Outputs:
- block_out: bfloat16 [2, 48, 64, 1280], P('dp', 'tm')
- grad_tokens: bfloat16 [2, 48, 64, 1280], P('dp', 'tm')
- grad_output_weight: float32 [640, 1280], P('tm')
The draws below stay inside these ranges and needn't reach their ends.
Inputs may be any that keep to these rules, and one draw needn't show every extreme that they name: visible[c, f, g] names which of the 3 cells of group g is visible in frame f.
All inputs are finite; a program needn't handle non-finite values.
Results may differ from the reference program's by a relative error of at most 0.012.
Values may be sent and summed in bfloat16 or wider, within the bound.
A program may use at most 64 MiB of HBM per device.

```python
import math
import jax
import jax.numpy as jnp
from jax import lax

D = 1280
HEADS = 8
HEAD_DIM = 80
ATT = 640
VIS = 64
GROUP_CELLS = 3
FRAMES = 48
CLIPS = 2


def draw_frame_tokens(key, part):
    noise = jax.random.normal(jax.random.fold_in(key, 31), (CLIPS, FRAMES, VIS, D), jnp.float32)
    return jnp.clip(noise, -7.5, 7.5).astype(jnp.bfloat16)


def query_key_pair(key):
    first = jax.random.normal(jax.random.fold_in(key, 41), (D, HEADS * HEAD_DIM), jnp.float32) / math.sqrt(D)
    second = jax.random.normal(jax.random.fold_in(key, 42), (D, HEADS * HEAD_DIM), jnp.float32) / math.sqrt(D)
    return (jnp.clip(first, -1.5, 1.5), jnp.clip(second, -1.5, 1.5))


def draw_query_weight(key, part):
    return query_key_pair(key)[0].astype(jnp.bfloat16)


def draw_key_weight(key, part):
    return query_key_pair(key)[1].astype(jnp.bfloat16)


def set_ends(array, rng, least, largest):
    shape = array.shape
    place = [jax.random.randint(jax.random.fold_in(rng, axis), (), 0, shape[axis]) for axis in range(len(shape))]
    array = array.at[tuple(place)].set(least)
    longest = shape.index(max(shape))
    place[longest] = (place[longest] + 1) % shape[longest]
    return array.at[tuple(place)].set(largest)


def with_spikes(values, key, source, target, parts, factor):
    def block_of(dim):
        return (jnp.arange(values.shape[dim]) // (values.shape[dim] // parts)).reshape((-1,) + (1,) * (values.ndim - 1 - dim))

    near = jax.random.permutation(key, parts)[block_of(target)]
    far = (block_of(target) + parts // 2) % parts
    return jnp.where((block_of(source) == near) | (block_of(source) == far), factor * values, values)


def level_of(own_key, dims, cuts, least, high):
    level = 1.0
    for axis_at, shards_of in cuts:
        steps = jax.random.uniform(jax.random.fold_in(jax.random.fold_in(own_key, 6), axis_at), (shards_of,), jnp.float32, least / len(cuts), high / len(cuts))
        level = level * jnp.repeat(jnp.exp(steps), dims[axis_at] // shards_of).reshape((-1,) + (1,) * (len(dims) - 1 - axis_at))
    return level


def gaussian(stream_key, extent, scale, most, pieces=(), held_as=jnp.bfloat16):
    values = jax.random.normal(stream_key, extent, jnp.float32) * scale
    if len(pieces) > 0:
        values = level_of(stream_key, extent, pieces, -0.22, 0.18) * values
    return jnp.clip(values, min=-most, max=most).astype(held_as)


def bell_draw_with(own_key, shape, scale, bound, pieces, heavy, kind=jnp.bfloat16):
    array = scale * jax.random.normal(own_key, shape, jnp.float32)
    if pieces:
        array = array * level_of(own_key, shape, pieces, -0.22, 0.18)
    return jnp.clip(with_spikes(array, jax.random.fold_in(own_key, 3), *heavy), -bound, bound).astype(kind)


def setup_inputs(seed: int = 0) -> dict:
    arg_keys = jax.random.split(jax.random.key(seed), 9)
    return {
        "frame_tokens": draw_frame_tokens(jax.random.fold_in(arg_keys[8], 71), 0),
        "visible": set_ends(jax.random.randint(arg_keys[1], (CLIPS, FRAMES, VIS), 0, GROUP_CELLS), jax.random.fold_in(arg_keys[1], 1), 0, GROUP_CELLS - 1).astype(jnp.int32),
        "grad_output": bell_draw_with(arg_keys[2], (CLIPS, FRAMES, VIS, D), 1.0, 6.0, ((0, 2), (1, 16)), (1, 3, 16, 2.0)),
        "norm_gain": jnp.clip(1.0 + 0.18 * jax.random.normal(arg_keys[3], (D,), jnp.float32), 0.1, 1.9),
        "query_weight": draw_query_weight(jax.random.fold_in(arg_keys[8], 71), 0),
        "key_weight": draw_key_weight(jax.random.fold_in(arg_keys[8], 71), 0),
        "value_weight": gaussian(arg_keys[6], (D, ATT), D ** -0.5, 0.15625, ((0, 16),)),
        "output_weight": gaussian(arg_keys[7], (ATT, D), ATT ** -0.5, 0.25, ((0, 16),)),
    }


NORM_EPS = 1e-06

def normalize(token_rows, norm_gain):
    values = token_rows.astype(jnp.float32)
    centered = values - lax.optimization_barrier(jnp.mean(values, axis=-1, keepdims=True))
    inverse = lax.rsqrt(lax.optimization_barrier(jnp.mean(centered * centered, axis=-1, keepdims=True)) + NORM_EPS)
    scaled = centered * inverse
    return (scaled, inverse, (scaled * norm_gain).astype(jnp.bfloat16))

def project(token_rows, weight):
    lead_shape = token_rows.shape[:-1]
    flat_rows = token_rows.reshape(-1, token_rows.shape[-1])
    result = jnp.dot(flat_rows, weight, preferred_element_type=jnp.float32)
    return result.astype(jnp.bfloat16).reshape(lead_shape + (weight.shape[1],))

def split_heads(values):
    return values.reshape(values.shape[:-1] + (HEADS, values.shape[-1] // HEADS)).astype(jnp.float32)

def attend(query_rows, key_rows, value_rows, same_cell):
    score_scale = 1.0 / jnp.sqrt(jnp.float32(HEAD_DIM))
    query_heads = split_heads(query_rows)
    key_heads = split_heads(key_rows)
    value_heads = split_heads(value_rows)
    scores = jnp.einsum('fghe,tghe->ghft', query_heads, key_heads) * score_scale
    scores = jnp.where(same_cell[:, None], scores, -jnp.inf)
    row_top = lax.optimization_barrier(jnp.max(scores, axis=-1, keepdims=True))
    expons = jnp.exp(scores - row_top)
    soft_probs = expons / lax.optimization_barrier(jnp.sum(expons, axis=-1, keepdims=True))
    probs_low = soft_probs.astype(jnp.bfloat16)
    mixed_rows = jnp.einsum('ghft,tghe->fghe', probs_low.astype(jnp.float32), value_heads)
    return (soft_probs, probs_low, mixed_rows.reshape(query_rows.shape).astype(jnp.bfloat16))

def attend_back(query_rows, key_rows, value_rows, soft_probs, probs_low, grad_mixed):
    score_scale = 1.0 / jnp.sqrt(jnp.float32(HEAD_DIM))
    query_heads = split_heads(query_rows)
    key_heads = split_heads(key_rows)
    value_heads = split_heads(value_rows)
    grad_heads = split_heads(grad_mixed)
    grad_probs = jnp.einsum('fghe,tghe->ghft', grad_heads, value_heads)
    centre = lax.optimization_barrier(jnp.sum(soft_probs * grad_probs, axis=-1, keepdims=True))
    grad_scores = (soft_probs * (grad_probs - centre) * score_scale).astype(jnp.bfloat16).astype(jnp.float32)
    grad_query = jnp.einsum('ghft,tghe->fghe', grad_scores, key_heads)
    grad_key = jnp.einsum('ghft,fghe->tghe', grad_scores, query_heads)
    grad_value = jnp.einsum('ghft,fghe->tghe', probs_low.astype(jnp.float32), grad_heads)
    full_shape = query_rows.shape
    return (grad_query.reshape(full_shape).astype(jnp.bfloat16), grad_key.reshape(full_shape).astype(jnp.bfloat16), grad_value.reshape(full_shape).astype(jnp.bfloat16))

def back_project(grad_query, grad_key, grad_value, query_weight, key_weight, value_weight):
    lead_shape = grad_query.shape[:-1]
    width = grad_query.shape[-1]
    total = jnp.dot(grad_query.reshape(-1, width), query_weight.T, preferred_element_type=jnp.float32)
    total = total + jnp.dot(grad_key.reshape(-1, width), key_weight.T, preferred_element_type=jnp.float32)
    total = total + jnp.dot(grad_value.reshape(-1, width), value_weight.T, preferred_element_type=jnp.float32)
    return total.astype(jnp.bfloat16).reshape(lead_shape + (query_weight.shape[0],))

def reference(frame_tokens, visible, grad_output, norm_gain, query_weight, key_weight, value_weight, output_weight):

    def one_clip(inputs):
        tokens, cells, grad_clip = inputs
        scaled, inverse, normed = normalize(tokens, norm_gain)
        query_rows = project(normed, query_weight)
        key_rows = project(normed, key_weight)
        value_rows = project(normed, value_weight)
        cell_major = cells.T
        same_cell = cell_major[:, :, None] == cell_major[:, None, :]
        soft_probs, probs_low, mixed_rows = attend(query_rows, key_rows, value_rows, same_cell)
        flat_mixed = mixed_rows.reshape(-1, mixed_rows.shape[-1])
        flat_tokens = tokens.reshape(-1, tokens.shape[-1])
        update = jnp.dot(flat_mixed, output_weight, preferred_element_type=jnp.float32)
        block_rows = (flat_tokens.astype(jnp.float32) + update).astype(jnp.bfloat16).reshape(tokens.shape)
        flat_grad = grad_clip.reshape(-1, grad_clip.shape[-1])
        grad_mixed = jnp.dot(flat_grad, output_weight.T, preferred_element_type=jnp.float32)
        grad_mixed = grad_mixed.astype(jnp.bfloat16).reshape(mixed_rows.shape)
        weight_term = jnp.dot(flat_mixed.T, flat_grad, preferred_element_type=jnp.float32)
        grad_query, grad_key, grad_value = attend_back(query_rows, key_rows, value_rows, soft_probs, probs_low, grad_mixed)
        grad_normed = back_project(grad_query, grad_key, grad_value, query_weight, key_weight, value_weight)
        weighted = grad_normed.astype(jnp.float32) * norm_gain
        first_mean = lax.optimization_barrier(jnp.mean(weighted, axis=-1, keepdims=True))
        second_mean = lax.optimization_barrier(jnp.mean(weighted * scaled, axis=-1, keepdims=True))
        grad_rows = inverse * (weighted - first_mean - scaled * second_mean) + grad_clip.astype(jnp.float32)
        return (block_rows, grad_rows.astype(jnp.bfloat16), weight_term)
    block_out, grad_tokens, weight_terms = lax.map(one_clip, (frame_tokens, visible, grad_output))
    return (block_out, grad_tokens, lax.optimization_barrier(jnp.sum(weight_terms, axis=0)))
```

```python
import math

import jax
import jax.numpy as jnp
from jax import lax
from jax.experimental import pallas as pl
from jax.experimental.pallas import tpu as pltpu
from jax.sharding import PartitionSpec as P

HEADS = 8


NORM_EPS = 1e-06


def normalize(token_rows, norm_gain):
    values = token_rows.astype(jnp.float32)
    centered = values - jnp.mean(values, axis=-1, keepdims=True)
    inverse = lax.rsqrt(jnp.mean(centered * centered, axis=-1, keepdims=True) + NORM_EPS)
    scaled = centered * inverse
    return (scaled, inverse, (scaled * norm_gain).astype(jnp.bfloat16))


def project(token_rows, weight):
    lead_shape = token_rows.shape[:-1]
    flat_rows = token_rows.reshape(-1, token_rows.shape[-1])
    result = jnp.dot(flat_rows, weight, preferred_element_type=jnp.float32)
    return result.astype(jnp.bfloat16).reshape(lead_shape + (weight.shape[1],))


def split_heads(values):
    return values.reshape(values.shape[:-1] + (HEADS, values.shape[-1] // HEADS))


def attend(query_rows, key_rows, value_rows, same_cell):
    score_scale = 1.0 / math.sqrt(query_rows.shape[-1] // HEADS)
    query_heads = split_heads(query_rows)
    key_heads = split_heads(key_rows)
    value_heads = split_heads(value_rows)
    scores = (
        jnp.einsum("fghe,tghe->ghft", query_heads, key_heads, preferred_element_type=jnp.float32)
        * score_scale
    )
    scores = jnp.where(same_cell[:, None], scores, -jnp.inf)
    row_top = jnp.max(scores, axis=-1, keepdims=True)
    expons = jnp.exp(scores - row_top)
    soft_probs = expons / jnp.sum(expons, axis=-1, keepdims=True)
    probs_low = soft_probs.astype(jnp.bfloat16)
    mixed_rows = jnp.einsum(
        "ghft,tghe->fghe", probs_low, value_heads, preferred_element_type=jnp.float32
    )
    return (soft_probs, probs_low, mixed_rows.reshape(query_rows.shape).astype(jnp.bfloat16))


def attend_back(query_rows, key_rows, value_rows, soft_probs, probs_low, grad_mixed):
    score_scale = 1.0 / math.sqrt(query_rows.shape[-1] // HEADS)
    query_heads = split_heads(query_rows)
    key_heads = split_heads(key_rows)
    value_heads = split_heads(value_rows)
    grad_heads = split_heads(grad_mixed)
    grad_probs = jnp.einsum(
        "fghe,tghe->ghft", grad_heads, value_heads, preferred_element_type=jnp.float32
    )
    centre = jnp.sum(soft_probs * grad_probs, axis=-1, keepdims=True)
    grad_scores = (soft_probs * (grad_probs - centre) * score_scale).astype(jnp.bfloat16)
    grad_query = jnp.einsum(
        "ghft,tghe->fghe", grad_scores, key_heads, preferred_element_type=jnp.float32
    )
    grad_key = jnp.einsum(
        "ghft,fghe->tghe", grad_scores, query_heads, preferred_element_type=jnp.float32
    )
    grad_value = jnp.einsum(
        "ghft,fghe->tghe", probs_low, grad_heads, preferred_element_type=jnp.float32
    )
    full_shape = query_rows.shape
    return (
        grad_query.reshape(full_shape).astype(jnp.bfloat16),
        grad_key.reshape(full_shape).astype(jnp.bfloat16),
        grad_value.reshape(full_shape).astype(jnp.bfloat16),
    )


def back_project(grad_query, grad_key, grad_value, query_weight, key_weight, value_weight):
    lead_shape = grad_query.shape[:-1]
    width = grad_query.shape[-1]
    total = jnp.dot(
        grad_query.reshape(-1, width), query_weight.T, preferred_element_type=jnp.float32
    )
    total = total + jnp.dot(
        grad_key.reshape(-1, width), key_weight.T, preferred_element_type=jnp.float32
    )
    total = total + jnp.dot(
        grad_value.reshape(-1, width), value_weight.T, preferred_element_type=jnp.float32
    )
    return total.astype(jnp.bfloat16).reshape(lead_shape + (query_weight.shape[0],))


def on_device(
    frame_tokens,
    visible,
    grad_output,
    norm_gain,
    query_weight,
    key_weight,
    value_weight,
    output_weight,
):
    query_weight, key_weight, value_weight, output_weight = (
        lax.all_gather(query_weight, "tm", axis=0, tiled=True),
        lax.all_gather(key_weight, "tm", axis=0, tiled=True),
        lax.all_gather(value_weight, "tm", axis=0, tiled=True),
        lax.all_gather(output_weight, "tm", axis=0, tiled=True),
    )
    shards = lax.axis_size("tm")
    tokens = frame_tokens[0]
    frame_count, visible_count, width = tokens.shape
    att_width = output_weight.shape[0]
    groups = visible_count // shards
    scaled, inverse, normed = normalize(tokens, norm_gain)
    local_cells = lax.dynamic_slice_in_dim(visible[0], lax.axis_index("tm") * groups, groups, 1)
    cell_major = local_cells.T
    same_cell = cell_major[:, :, None] == cell_major[:, None, :]
    query_rows = project(normed, query_weight)
    key_rows = project(normed, key_weight)
    value_rows = project(normed, value_weight)
    query_rows, key_rows, value_rows = (
        lax.all_to_all(query_rows, "tm", split_axis=1, concat_axis=0, tiled=True),
        lax.all_to_all(key_rows, "tm", split_axis=1, concat_axis=0, tiled=True),
        lax.all_to_all(value_rows, "tm", split_axis=1, concat_axis=0, tiled=True),
    )
    soft_probs, probs_low, mixed_cells = attend(query_rows, key_rows, value_rows, same_cell)
    mixed_frames = lax.all_to_all(mixed_cells, "tm", split_axis=0, concat_axis=1, tiled=True)
    flat_mixed = mixed_frames.reshape(-1, att_width)
    flat_tokens = tokens.reshape(-1, width)
    update = jnp.dot(flat_mixed, output_weight, preferred_element_type=jnp.float32)
    block_rows = (
        (flat_tokens.astype(jnp.float32) + update).astype(jnp.bfloat16).reshape(tokens.shape)
    )
    flat_grad = grad_output[0].reshape(-1, width)
    grad_mixed = jnp.dot(flat_grad, output_weight.T, preferred_element_type=jnp.float32)
    grad_mixed = grad_mixed.astype(jnp.bfloat16).reshape(frame_count, visible_count, att_width)
    term_share = lax.psum_scatter(
        jnp.dot(flat_mixed.T, flat_grad, preferred_element_type=jnp.float32),
        "tm",
        scatter_dimension=0,
        tiled=True,
    )
    grad_weight = lax.psum(term_share.astype(jnp.bfloat16), "dp").astype(jnp.float32)
    grad_cells = lax.all_to_all(grad_mixed, "tm", split_axis=1, concat_axis=0, tiled=True)
    grad_query, grad_key, grad_value = attend_back(
        query_rows, key_rows, value_rows, soft_probs, probs_low, grad_cells
    )
    grad_query, grad_key, grad_value = (
        lax.all_to_all(grad_query, "tm", split_axis=0, concat_axis=1, tiled=True),
        lax.all_to_all(grad_key, "tm", split_axis=0, concat_axis=1, tiled=True),
        lax.all_to_all(grad_value, "tm", split_axis=0, concat_axis=1, tiled=True),
    )
    grad_normed = back_project(
        grad_query, grad_key, grad_value, query_weight, key_weight, value_weight
    )
    weighted = grad_normed.astype(jnp.float32) * norm_gain
    first_mean = jnp.mean(weighted, axis=-1, keepdims=True)
    second_mean = jnp.mean(weighted * scaled, axis=-1, keepdims=True)
    grad_rows = inverse * (weighted - first_mean - scaled * second_mean) + grad_output[0].astype(
        jnp.float32
    )
    return (block_rows[None], grad_rows.astype(jnp.bfloat16)[None], grad_weight)


SHARDS = 16
ROWS = 16


def nt_dot(left, right):
    return lax.dot_general(left, right, (((1,), (1,)), ((), ())), preferred_element_type=jnp.float32)


def tn_dot(left, right):
    return lax.dot_general(left, right, (((0,), (0,)), ((), ())), preferred_element_type=jnp.float32)


def nn_dot(left, right):
    return jnp.dot(left, right, preferred_element_type=jnp.float32)


def head_window(head, head_dim):
    low = head * head_dim
    start = low // 128 * 128
    stop = -(-(low + head_dim) // 128) * 128
    lane = lax.broadcasted_iota(jnp.int32, (1, stop - start), 1) + start
    inside = jnp.where((lane >= low) & (lane < low + head_dim), 1.0, 0.0)
    return (slice(start, stop), inside.astype(jnp.bfloat16))


def fused_kernel(
    tok, gout, gain, code_col, code_row, w4,
    block_o, gtok_o, dw_o,
    wall, norm_s, norm_r, gout_r, q_s, k_s, v_s, gm_s, probs_s,
    acc_a, acc_b, acc_c, mix_s, mix_r, gn_s, gn_r,
    dwp, dw_in, dwc_s, dwc_r, dwf,
    w_send, w_recv, sib_send, sib_recv, go_send, go_recv, no_send, no_recv,
    mi_send, mi_recv, gn_send, gn_recv, dw_send, dw_recv, pair_send, pair_recv,
):
    t = lax.axis_index("tm")
    c = lax.axis_index("dp")
    x = lax.rem(t, 2)
    y = lax.rem(lax.div(t, 2), 2)
    z = lax.div(t, 4)
    plane = lax.rem(t, 4)
    xn = t + 1 - 2 * x
    yn = t + 2 - 4 * y
    att = q_s.shape[1]
    head_dim = att // HEADS
    scale = 1.0 / math.sqrt(head_dim)
    half = pl.ds(2 * c, 2)

    def to_tm(src, dst, send, recv, peer):
        return pltpu.make_async_remote_copy(
            src_ref=src, dst_ref=dst, send_sem=send, recv_sem=recv,
            device_id={"tm": peer}, device_id_type=pl.DeviceIdType.MESH,
        )

    def to_pair(src, dst, send, recv):
        return pltpu.make_async_remote_copy(
            src_ref=src, dst_ref=dst, send_sem=send, recv_sem=recv,
            device_id={"dp": 1 - c}, device_id_type=pl.DeviceIdType.MESH,
        )

    barrier = pltpu.get_barrier_semaphore()

    @pl.loop(1, SHARDS)
    def _(d):
        pl.semaphore_signal(
            barrier, inc=1, device_id={"tm": lax.rem(t + d, SHARDS)},
            device_id_type=pl.DeviceIdType.MESH,
        )

    pl.semaphore_signal(
        barrier, inc=1, device_id={"dp": 1 - c}, device_id_type=pl.DeviceIdType.MESH
    )
    pl.semaphore_wait(barrier, SHARDS)

    def item(s):
        return wall.at[half, s]

    def own_item(peer, slot):
        return to_tm(w4.at[half], item(t), w_send.at[slot], w_recv.at[t], peer)

    for slot, peer in ((3, xn), (7, yn)):
        own_item(peer, slot).start()
    for i in range(1, 4):
        own_item(lax.rem(z + i, 4) * 4 + plane, i - 1).start()

    def peer_copy(src, dst, send, recv, peer):
        return to_tm(src.at[peer], dst.at[t], send.at[peer], recv.at[t], peer)

    def wait_peers(src, dst, send, recv, sends):
        @pl.loop(1, SHARDS)
        def _(d):
            peer = lax.rem(t + d, SHARDS)
            if sends:
                peer_copy(src, dst, send, recv, peer).wait_send()
            else:
                to_tm(src.at[peer], dst.at[peer], send.at[peer], recv.at[peer], peer).wait_recv()

    @pl.loop(1, SHARDS)
    def _(d):
        peer_copy(gout, gout_r, go_send, go_recv, lax.rem(t + d, SHARDS)).start()

    def norm_block(p):
        values = tok[p].astype(jnp.float32)
        centered = values - jnp.mean(values, axis=-1, keepdims=True)
        inverse = lax.rsqrt(jnp.mean(centered * centered, axis=-1, keepdims=True) + NORM_EPS)
        return (centered * inverse, inverse)

    @pl.loop(1, SHARDS + 1)
    def _(d):
        peer = lax.rem(t + d, SHARDS)
        norm_s[peer] = (norm_block(peer)[0] * gain[...]).astype(jnp.bfloat16)

        @pl.when(d < SHARDS)
        def _():
            peer_copy(norm_s, norm_r, no_send, no_recv, peer).start()

    norm_r[t] = norm_s[t]
    gout_r[t] = gout[t]
    for j in range(4):
        wall[j, t] = w4[j]

    def wait_item(s):
        to_tm(item(s), item(s), w_send.at[0], w_recv.at[s], xn).wait_recv()

    def pass_item(s, peer, slot):
        return to_tm(item(s), item(s), w_send.at[slot], w_recv.at[s], peer)

    def pair_item(s):
        return to_pair(item(s), item(s), sib_send.at[s], sib_recv.at[s])

    for i in range(4):
        level = lax.rem(z + 4 - i, 4) * 4
        mine = level + plane
        if i > 0:
            wait_item(mine)
            pass_item(mine, xn, 3 + i).start()
            pass_item(mine, yn, 7 + i).start()
            pair_item(mine).start()
    for i in range(4):
        level = lax.rem(z + 4 - i, 4) * 4
        from_x = level + lax.rem(xn, 4)
        from_y = level + lax.rem(yn, 4)

        wait_item(from_x)

        @pl.when(c == 0)
        def _():
            pass_item(from_x, yn, 11 + i).start()

        pair_item(from_x).start()
        wait_item(from_y)

        @pl.when(c == 1)
        def _():
            pass_item(from_y, xn, 11 + i).start()

        pair_item(from_y).start()
    for i in range(4):
        level = lax.rem(z + 4 - i, 4) * 4
        across = level + 3 - plane
        wait_item(across)
        pair_item(across).start()

    wait_peers(norm_s, norm_r, no_send, no_recv, False)
    wait_peers(gout, gout_r, go_send, go_recv, False)

    other = pl.ds(2 - 2 * c, 2)

    @pl.loop(1, SHARDS)
    def _(d):
        s = lax.rem(t + d, SHARDS)
        to_pair(
            wall.at[other, s], wall.at[other, s], sib_send.at[s], sib_recv.at[s]
        ).wait_recv()

    width = tok.shape[2]
    depth = w4.shape[1]
    rows = SHARDS * ROWS

    def full(j):
        return wall[j].reshape(SHARDS * depth, att)

    share = depth // 2

    def output_half(j):
        blocks = wall[3].astype(jnp.float32)[:, j * share : (j + 1) * share]
        return blocks.reshape(SHARDS * share, att).astype(jnp.bfloat16)

    normed = norm_r[...].reshape(rows, width)
    grads = gout_r[...].reshape(rows, width)
    q_s[...] = nn_dot(normed, full(0)).astype(jnp.bfloat16)
    k_s[...] = nn_dot(normed, full(1)).astype(jnp.bfloat16)
    v_s[...] = nn_dot(normed, full(2)).astype(jnp.bfloat16)

    same = code_col[...] == code_row[...]
    acc_a[...] = jnp.zeros_like(acc_a)
    for head in range(HEADS):
        window, inside = head_window(head, head_dim)
        scores = nt_dot(q_s[:, window] * inside, k_s[:, window]) * scale
        scores = jnp.where(same, scores, -jnp.inf)
        expons = jnp.exp(scores - jnp.max(scores, axis=-1, keepdims=True))
        probs = expons / jnp.sum(expons, axis=-1, keepdims=True)
        probs_s[head] = probs
        acc_a[:, window] += nn_dot(probs.astype(jnp.bfloat16), v_s[:, window] * inside)
    mix_s[...] = acc_a[...].astype(jnp.bfloat16).reshape(SHARDS, ROWS, att)

    @pl.loop(1, SHARDS)
    def _(d):
        peer_copy(mix_s, mix_r, mi_send, mi_recv, lax.rem(t + d, SHARDS)).start()

    mix_r[t] = mix_s[t]

    mixed = mix_s[...].reshape(rows, att)
    for j in range(2):
        term = tn_dot(mixed, grads[:, j * att : (j + 1) * att])
        dwp[j] = term.reshape(SHARDS, share, att).astype(jnp.bfloat16)
    pair_term = to_pair(dwp.at[1 - c], dw_in, pair_send.at[0], pair_recv.at[0])
    pair_term.start()

    gm_s[:, :] = (
        nt_dot(grads[:, :att], output_half(0)) + nt_dot(grads[:, att:], output_half(1))
    ).astype(jnp.bfloat16)

    pair_term.wait_recv()

    @pl.loop(1, SHARDS + 1)
    def _(d):
        peer = lax.rem(t + d, SHARDS)
        total = dwp[c, peer].astype(jnp.float32) + dw_in[peer].astype(jnp.float32)
        dwc_s[peer] = total.astype(jnp.bfloat16)

        @pl.when(d < SHARDS)
        def _():
            peer_copy(dwc_s, dwc_r, dw_send, dw_recv, peer).start()

    dwc_r[t] = dwc_s[t]

    acc_a[...] = jnp.zeros_like(acc_a)
    acc_b[...] = jnp.zeros_like(acc_b)
    acc_c[...] = jnp.zeros_like(acc_c)
    for head in range(HEADS):
        window, inside = head_window(head, head_dim)
        grad_head = gm_s[:, window] * inside
        probs = probs_s[head]
        grad_probs = nt_dot(grad_head, v_s[:, window])
        centre = jnp.sum(probs * grad_probs, axis=-1, keepdims=True)
        grad_scores = (probs * (grad_probs - centre) * scale).astype(jnp.bfloat16)
        acc_a[:, window] += nn_dot(grad_scores, k_s[:, window] * inside)
        acc_b[:, window] += tn_dot(grad_scores, q_s[:, window] * inside)
        acc_c[:, window] += tn_dot(probs.astype(jnp.bfloat16), grad_head)
    total = nt_dot(acc_a[...].astype(jnp.bfloat16), full(0))
    total += nt_dot(acc_b[...].astype(jnp.bfloat16), full(1))
    total += nt_dot(acc_c[...].astype(jnp.bfloat16), full(2))
    gn_s[...] = total.astype(jnp.bfloat16).reshape(SHARDS, ROWS, width)

    @pl.loop(1, SHARDS)
    def _(d):
        peer_copy(gn_s, gn_r, gn_send, gn_recv, lax.rem(t + d, SHARDS)).start()

    gn_r[t] = gn_s[t]

    wait_peers(mix_s, mix_r, mi_send, mi_recv, False)
    mixed_frames = mix_r[...].reshape(rows, att)
    for j in range(2):
        columns = slice(j * att, (j + 1) * att)
        update = nn_dot(mixed_frames, output_half(j)).reshape(SHARDS, ROWS, att)
        block_o[:, :, columns] = (tok[:, :, columns].astype(jnp.float32) + update).astype(
            jnp.bfloat16
        )

    wait_peers(dwc_s, dwc_r, dw_send, dw_recv, False)
    dwf[c] = jnp.sum(dwc_r[...].astype(jnp.float32), axis=0)
    pair_sum = to_pair(dwf.at[c], dwf.at[c], pair_send.at[1], pair_recv.at[1])
    pair_sum.start()

    wait_peers(gn_s, gn_r, gn_send, gn_recv, False)

    @pl.loop(0, SHARDS)
    def _(p):
        scaled, inverse = norm_block(p)
        weighted = gn_r[p].astype(jnp.float32) * gain[...]
        first = jnp.mean(weighted, axis=-1, keepdims=True)
        second = jnp.mean(weighted * scaled, axis=-1, keepdims=True)
        result = inverse * (weighted - first - scaled * second) + gout[p].astype(jnp.float32)
        gtok_o[p] = result.astype(jnp.bfloat16)

    to_pair(dwf.at[1 - c], dwf.at[1 - c], pair_send.at[1], pair_recv.at[1]).wait_recv()
    dw_o[...] = dwf[...]

    pair_term.wait_send()
    pair_sum.wait_send()
    for slot in range(15):
        pass_item(t, xn, slot).wait_send()

    @pl.loop(1, SHARDS)
    def _(d):
        pair_item(lax.rem(t + d, SHARDS)).wait_send()

    wait_peers(gout, gout_r, go_send, go_recv, True)
    wait_peers(norm_s, norm_r, no_send, no_recv, True)
    wait_peers(mix_s, mix_r, mi_send, mi_recv, True)
    wait_peers(dwc_s, dwc_r, dw_send, dw_recv, True)
    wait_peers(gn_s, gn_r, gn_send, gn_recv, True)


def to_blocks(rows):
    frames, cells, width = rows.shape
    groups = cells // SHARDS
    blocks = rows.reshape(frames, SHARDS, groups, width).transpose(1, 0, 2, 3)
    blocks = blocks.reshape(SHARDS, frames * groups, width)
    return jnp.pad(blocks, ((0, 0), (0, ROWS - frames * groups), (0, 0)))


def from_blocks(blocks, shape):
    frames, cells, width = shape
    groups = cells // SHARDS
    rows = blocks[:, : frames * groups].reshape(SHARDS, frames, groups, width)
    return rows.transpose(1, 0, 2, 3).reshape(shape)


def on_chip_grid(
    frame_tokens,
    visible,
    grad_output,
    norm_gain,
    query_weight,
    key_weight,
    value_weight,
    output_weight,
):
    tokens = frame_tokens[0]
    frames, cells, width = tokens.shape
    groups = cells // SHARDS
    depth, att = query_weight.shape
    share = output_weight.shape[0]
    local = lax.dynamic_slice_in_dim(visible[0], lax.axis_index("tm") * groups, groups, 1)
    codes = local + 4 * jnp.arange(groups, dtype=jnp.int32)[None]
    codes = jnp.pad(
        codes.reshape(SHARDS, frames * groups),
        ((0, 0), (0, ROWS - frames * groups)),
        constant_values=-1,
    )
    output_rows = jnp.concatenate([output_weight[:, :att], output_weight[:, att:]], axis=0)
    stacked = jnp.stack([query_weight, key_weight, value_weight, output_rows])
    rows = SHARDS * ROWS
    low, high = jnp.bfloat16, jnp.float32
    vmem = pl.BlockSpec(memory_space=pltpu.VMEM)
    dma = pltpu.SemaphoreType.DMA
    block_rows, grad_rows, grad_weight = pl.pallas_call(
        fused_kernel,
        out_shape=(
            jax.ShapeDtypeStruct((SHARDS, ROWS, width), low),
            jax.ShapeDtypeStruct((SHARDS, ROWS, width), low),
            jax.ShapeDtypeStruct((2, share, att), high),
        ),
        in_specs=[vmem] * 6,
        out_specs=(vmem,) * 3,
        scratch_shapes=[
            pltpu.VMEM((4, SHARDS, depth, att), low),
            pltpu.VMEM((SHARDS, ROWS, width), low),
            pltpu.VMEM((SHARDS, ROWS, width), low),
            pltpu.VMEM((SHARDS, ROWS, width), low),
            pltpu.VMEM((rows, att), low),
            pltpu.VMEM((rows, att), low),
            pltpu.VMEM((rows, att), low),
            pltpu.VMEM((rows, att), low),
            pltpu.VMEM((HEADS, rows, rows), high),
            pltpu.VMEM((rows, att), high),
            pltpu.VMEM((rows, att), high),
            pltpu.VMEM((rows, att), high),
            pltpu.VMEM((SHARDS, ROWS, att), low),
            pltpu.VMEM((SHARDS, ROWS, att), low),
            pltpu.VMEM((SHARDS, ROWS, width), low),
            pltpu.VMEM((SHARDS, ROWS, width), low),
            pltpu.VMEM((2, SHARDS, share, att), low),
            pltpu.VMEM((SHARDS, share, att), low),
            pltpu.VMEM((SHARDS, share, att), low),
            pltpu.VMEM((SHARDS, share, att), low),
            pltpu.VMEM((2, share, att), high),
            dma((15,)),
            *[dma((SHARDS,))] * 13,
            dma((2,)),
            dma((2,)),
        ],
        compiler_params=pltpu.CompilerParams(
            collective_id=0, has_side_effects=True, vmem_limit_bytes=56 * 1024 * 1024
        ),
        name="temporal_block",
    )(
        to_blocks(tokens),
        to_blocks(grad_output[0]),
        norm_gain[None],
        codes.reshape(rows, 1),
        codes.reshape(1, rows),
        stacked,
    )
    grad_weight = jnp.concatenate([grad_weight[0], grad_weight[1]], axis=1)
    return (
        from_blocks(block_rows, tokens.shape)[None],
        from_blocks(grad_rows, tokens.shape)[None],
        grad_weight,
    )


def solution(mesh):
    chip_grid = mesh.shape["tm"] == SHARDS and mesh.shape["dp"] == 2
    return jax.shard_map(
        on_chip_grid if chip_grid else on_device,
        mesh=mesh,
        in_specs=(
            P("dp", "tm", None, None),
            P("dp", None, None),
            P("dp", "tm", None, None),
            P(),
            P("tm", None),
            P("tm", None),
            P("tm", None),
            P("tm", None),
        ),
        out_specs=(P("dp", "tm", None, None), P("dp", "tm", None, None), P("tm", None)),
        check_vma=False,
    )
```

```python
import math

import jax
import jax.numpy as jnp
from jax import lax
from jax.experimental import pallas as pl
from jax.experimental.pallas import tpu as pltpu
from jax.sharding import PartitionSpec as P

HEADS = 8


NORM_EPS = 1e-06


def normalize(token_rows, norm_gain):
    values = token_rows.astype(jnp.float32)
    centered = values - jnp.mean(values, axis=-1, keepdims=True)
    inverse = lax.rsqrt(jnp.mean(centered * centered, axis=-1, keepdims=True) + NORM_EPS)
    scaled = centered * inverse
    return (scaled, inverse, (scaled * norm_gain).astype(jnp.bfloat16))


def project(token_rows, weight):
    lead_shape = token_rows.shape[:-1]
    flat_rows = token_rows.reshape(-1, token_rows.shape[-1])
    result = jnp.dot(flat_rows, weight, preferred_element_type=jnp.float32)
    return result.astype(jnp.bfloat16).reshape(lead_shape + (weight.shape[1],))


def split_heads(values):
    return values.reshape(values.shape[:-1] + (HEADS, values.shape[-1] // HEADS))


def attend(query_rows, key_rows, value_rows, same_cell):
    score_scale = 1.0 / math.sqrt(query_rows.shape[-1] // HEADS)
    query_heads = split_heads(query_rows)
    key_heads = split_heads(key_rows)
    value_heads = split_heads(value_rows)
    scores = (
        jnp.einsum("fghe,tghe->ghft", query_heads, key_heads, preferred_element_type=jnp.float32)
        * score_scale
    )
    scores = jnp.where(same_cell[:, None], scores, -jnp.inf)
    row_top = jnp.max(scores, axis=-1, keepdims=True)
    expons = jnp.exp(scores - row_top)
    soft_probs = expons / jnp.sum(expons, axis=-1, keepdims=True)
    probs_low = soft_probs.astype(jnp.bfloat16)
    mixed_rows = jnp.einsum(
        "ghft,tghe->fghe", probs_low, value_heads, preferred_element_type=jnp.float32
    )
    return (soft_probs, probs_low, mixed_rows.reshape(query_rows.shape).astype(jnp.bfloat16))


def attend_back(query_rows, key_rows, value_rows, soft_probs, probs_low, grad_mixed):
    score_scale = 1.0 / math.sqrt(query_rows.shape[-1] // HEADS)
    query_heads = split_heads(query_rows)
    key_heads = split_heads(key_rows)
    value_heads = split_heads(value_rows)
    grad_heads = split_heads(grad_mixed)
    grad_probs = jnp.einsum(
        "fghe,tghe->ghft", grad_heads, value_heads, preferred_element_type=jnp.float32
    )
    centre = jnp.sum(soft_probs * grad_probs, axis=-1, keepdims=True)
    grad_scores = (soft_probs * (grad_probs - centre) * score_scale).astype(jnp.bfloat16)
    grad_query = jnp.einsum(
        "ghft,tghe->fghe", grad_scores, key_heads, preferred_element_type=jnp.float32
    )
    grad_key = jnp.einsum(
        "ghft,fghe->tghe", grad_scores, query_heads, preferred_element_type=jnp.float32
    )
    grad_value = jnp.einsum(
        "ghft,fghe->tghe", probs_low, grad_heads, preferred_element_type=jnp.float32
    )
    full_shape = query_rows.shape
    return (
        grad_query.reshape(full_shape).astype(jnp.bfloat16),
        grad_key.reshape(full_shape).astype(jnp.bfloat16),
        grad_value.reshape(full_shape).astype(jnp.bfloat16),
    )


def back_project(grad_query, grad_key, grad_value, query_weight, key_weight, value_weight):
    lead_shape = grad_query.shape[:-1]
    width = grad_query.shape[-1]
    total = jnp.dot(
        grad_query.reshape(-1, width), query_weight.T, preferred_element_type=jnp.float32
    )
    total = total + jnp.dot(
        grad_key.reshape(-1, width), key_weight.T, preferred_element_type=jnp.float32
    )
    total = total + jnp.dot(
        grad_value.reshape(-1, width), value_weight.T, preferred_element_type=jnp.float32
    )
    return total.astype(jnp.bfloat16).reshape(lead_shape + (query_weight.shape[0],))


def on_device(
    frame_tokens,
    visible,
    grad_output,
    norm_gain,
    query_weight,
    key_weight,
    value_weight,
    output_weight,
):
    query_weight, key_weight, value_weight, output_weight = (
        lax.all_gather(query_weight, "tm", axis=0, tiled=True),
        lax.all_gather(key_weight, "tm", axis=0, tiled=True),
        lax.all_gather(value_weight, "tm", axis=0, tiled=True),
        lax.all_gather(output_weight, "tm", axis=0, tiled=True),
    )
    shards = lax.axis_size("tm")
    tokens = frame_tokens[0]
    frame_count, visible_count, width = tokens.shape
    att_width = output_weight.shape[0]
    groups = visible_count // shards
    scaled, inverse, normed = normalize(tokens, norm_gain)
    local_cells = lax.dynamic_slice_in_dim(visible[0], lax.axis_index("tm") * groups, groups, 1)
    cell_major = local_cells.T
    same_cell = cell_major[:, :, None] == cell_major[:, None, :]
    query_rows = project(normed, query_weight)
    key_rows = project(normed, key_weight)
    value_rows = project(normed, value_weight)
    query_rows, key_rows, value_rows = (
        lax.all_to_all(query_rows, "tm", split_axis=1, concat_axis=0, tiled=True),
        lax.all_to_all(key_rows, "tm", split_axis=1, concat_axis=0, tiled=True),
        lax.all_to_all(value_rows, "tm", split_axis=1, concat_axis=0, tiled=True),
    )
    soft_probs, probs_low, mixed_cells = attend(query_rows, key_rows, value_rows, same_cell)
    mixed_frames = lax.all_to_all(mixed_cells, "tm", split_axis=0, concat_axis=1, tiled=True)
    flat_mixed = mixed_frames.reshape(-1, att_width)
    flat_tokens = tokens.reshape(-1, width)
    update = jnp.dot(flat_mixed, output_weight, preferred_element_type=jnp.float32)
    block_rows = (
        (flat_tokens.astype(jnp.float32) + update).astype(jnp.bfloat16).reshape(tokens.shape)
    )
    flat_grad = grad_output[0].reshape(-1, width)
    grad_mixed = jnp.dot(flat_grad, output_weight.T, preferred_element_type=jnp.float32)
    grad_mixed = grad_mixed.astype(jnp.bfloat16).reshape(frame_count, visible_count, att_width)
    term_share = lax.psum_scatter(
        jnp.dot(flat_mixed.T, flat_grad, preferred_element_type=jnp.float32),
        "tm",
        scatter_dimension=0,
        tiled=True,
    )
    grad_weight = lax.psum(term_share.astype(jnp.bfloat16), "dp").astype(jnp.float32)
    grad_cells = lax.all_to_all(grad_mixed, "tm", split_axis=1, concat_axis=0, tiled=True)
    grad_query, grad_key, grad_value = attend_back(
        query_rows, key_rows, value_rows, soft_probs, probs_low, grad_cells
    )
    grad_query, grad_key, grad_value = (
        lax.all_to_all(grad_query, "tm", split_axis=0, concat_axis=1, tiled=True),
        lax.all_to_all(grad_key, "tm", split_axis=0, concat_axis=1, tiled=True),
        lax.all_to_all(grad_value, "tm", split_axis=0, concat_axis=1, tiled=True),
    )
    grad_normed = back_project(
        grad_query, grad_key, grad_value, query_weight, key_weight, value_weight
    )
    weighted = grad_normed.astype(jnp.float32) * norm_gain
    first_mean = jnp.mean(weighted, axis=-1, keepdims=True)
    second_mean = jnp.mean(weighted * scaled, axis=-1, keepdims=True)
    grad_rows = inverse * (weighted - first_mean - scaled * second_mean) + grad_output[0].astype(
        jnp.float32
    )
    return (block_rows[None], grad_rows.astype(jnp.bfloat16)[None], grad_weight)


SHARDS = 16
ROWS = 16


def nt_dot(left, right):
    return lax.dot_general(left, right, (((1,), (1,)), ((), ())), preferred_element_type=jnp.float32)


def tn_dot(left, right):
    return lax.dot_general(left, right, (((0,), (0,)), ((), ())), preferred_element_type=jnp.float32)


def nn_dot(left, right):
    return jnp.dot(left, right, preferred_element_type=jnp.float32)


def head_window(head, head_dim):
    low = head * head_dim
    start = low // 128 * 128
    stop = -(-(low + head_dim) // 128) * 128
    lane = lax.broadcasted_iota(jnp.int32, (1, stop - start), 1) + start
    inside = jnp.where((lane >= low) & (lane < low + head_dim), 1.0, 0.0)
    return (slice(start, stop), inside.astype(jnp.bfloat16))


def block_maps(cells, frames, row_map, tail_map):
    groups = cells // SHARDS
    taken = frames * groups
    rows = SHARDS * ROWS
    place = lax.broadcasted_iota(jnp.int32, (rows, frames * cells), 0)
    source = lax.broadcasted_iota(jnp.int32, (rows, frames * cells), 1)
    owner, inner = lax.div(place, ROWS), lax.rem(place, ROWS)
    wanted = lax.div(inner, groups) * cells + owner * groups + lax.rem(inner, groups)
    main = (inner < taken) & (source == wanted)
    row_map[0] = jnp.where(main, 1.0, 0.0).astype(jnp.bfloat16)
    for frame in range(frames):
        tail = (inner >= taken) & (source == frame * cells + owner * groups + inner - taken)
        row_map[1 + frame] = jnp.where(tail, 1.0, 0.0).astype(jnp.bfloat16)
    place = lax.broadcasted_iota(jnp.int32, (rows, rows), 0)
    source = lax.broadcasted_iota(jnp.int32, (rows, rows), 1)
    inner = lax.rem(place, ROWS)
    wanted = place - inner + taken + lax.rem(inner, groups)
    for frame in range(frames):
        hit = (lax.div(inner, groups) == frame) & (source == wanted)
        tail_map[frame] = jnp.where(hit, 1.0, 0.0).astype(jnp.bfloat16)


def fused_kernel(
    tok, gout, gain, code_row, wq, wk, wv, wo,
    block_o, gtok_o, dw_o,
    wall, row_map, tail_map, norm_s, norm_r, go_s, go_r, grad_b, q_s, k_s, v_s, gm_s, probs_s,
    acc_a, acc_b, acc_c, mix_b, mix_s, mix_r, gn_s, gn_r,
    dwp, dw_in, dwa_s, dwa_r, dwb_s, dwb_r, dwf,
    w_send, w_recv, sib_send, sib_recv, go_send, go_recv, no_send, no_recv,
    mi_send, mi_recv, gn_send, gn_recv, da_send, da_recv, db_send, db_recv, pair_send, pair_recv,
):
    t = lax.axis_index("tm")
    c = lax.axis_index("dp")
    x = lax.rem(t, 2)
    y = lax.rem(lax.div(t, 2), 2)
    z = lax.div(t, 4)
    plane = lax.rem(t, 4)
    xn = t + 1 - 2 * x
    yn = t + 2 - 4 * y
    att = q_s.shape[1]
    frames, cells, width = tok.shape
    count = frames * cells
    depth = wq.shape[0]
    share = wo.shape[0]
    rows = SHARDS * ROWS
    head_dim = att // HEADS
    scale = 1.0 / math.sqrt(head_dim)
    half = pl.ds(2 * c, 2)
    low, high = jnp.bfloat16, jnp.float32

    def to_tm(src, dst, send, recv, peer):
        return pltpu.make_async_remote_copy(
            src_ref=src, dst_ref=dst, send_sem=send, recv_sem=recv,
            device_id={"tm": peer}, device_id_type=pl.DeviceIdType.MESH,
        )

    def to_pair(src, dst, send, recv):
        return pltpu.make_async_remote_copy(
            src_ref=src, dst_ref=dst, send_sem=send, recv_sem=recv,
            device_id={"dp": 1 - c}, device_id_type=pl.DeviceIdType.MESH,
        )

    barrier = pltpu.get_barrier_semaphore()

    @pl.loop(1, SHARDS)
    def _(d):
        pl.semaphore_signal(
            barrier, inc=1, device_id={"tm": lax.rem(t + d, SHARDS)},
            device_id_type=pl.DeviceIdType.MESH,
        )

    pl.semaphore_signal(
        barrier, inc=1, device_id={"dp": 1 - c}, device_id_type=pl.DeviceIdType.MESH
    )
    wall[0, t] = wq[...]
    wall[1, t] = wk[...]
    wall[2, t] = wv[...]
    output_rows = wo[...].astype(high)
    wall[3, t] = jnp.concatenate([output_rows[:, :att], output_rows[:, att:]], axis=0).astype(low)
    pl.semaphore_wait(barrier, SHARDS)

    def item(s):
        return wall.at[half, s]

    def pass_item(s, peer, slot):
        return to_tm(item(s), item(s), w_send.at[slot], w_recv.at[s], peer)

    def wait_item(s):
        pass_item(s, xn, 0).wait_recv()

    def pair_item(s):
        return to_pair(item(s), item(s), sib_send.at[s], sib_recv.at[s])

    for slot, peer in ((3, xn), (7, yn)):
        pass_item(t, peer, slot).start()
    for i in range(1, 4):
        pass_item(t, lax.rem(z + i, 4) * 4 + plane, i - 1).start()

    def peer_copy(src, dst, send, recv, peer):
        return to_tm(src.at[peer], dst.at[t], send.at[peer], recv.at[t], peer)

    def send_peers(src, dst, send, recv):
        @pl.loop(1, SHARDS)
        def _(d):
            peer_copy(src, dst, send, recv, lax.rem(t + d, SHARDS)).start()

        dst[t] = src[t]

    def wait_peers(src, dst, send, recv, sends):
        @pl.loop(1, SHARDS)
        def _(d):
            peer = lax.rem(t + d, SHARDS)
            if sends:
                peer_copy(src, dst, send, recv, peer).wait_send()
            else:
                to_tm(src.at[peer], dst.at[peer], send.at[peer], recv.at[peer], peer).wait_recv()

    block_maps(cells, frames, row_map, tail_map)

    def pack_frames(values, out):
        columns = values.shape[1]
        tail = columns // 5
        packed = nn_dot(row_map[0], values[:, : columns - tail])
        spare = [nn_dot(row_map[1 + f], values[:, columns - tail :]) for f in range(frames)]
        spare.append(jnp.zeros((rows, columns - tail - frames * tail), high))
        packed = packed + jnp.concatenate(spare, axis=1)
        out[...] = packed.astype(low).reshape(out.shape)

    def pack_cells(values, out):
        columns = values.shape[1]
        tail = columns // 5
        spare = [tn_dot(tail_map[f], values[:, columns - tail :]) for f in range(frames)]
        spare.append(jnp.zeros((rows, columns - tail - frames * tail), high))
        packed = values[:, : columns - tail].astype(high) + jnp.concatenate(spare, axis=1)
        out[...] = packed.astype(low).reshape(out.shape)

    def unpack_frames(packed):
        columns = packed.shape[2] * 5 // 4
        tail = columns // 5
        values = packed[...].reshape(rows, columns - tail)
        main = tn_dot(row_map[0], values)
        last = sum(tn_dot(row_map[1 + f], values[:, f * tail : (f + 1) * tail]) for f in range(frames))
        return jnp.concatenate([main, last], axis=1)

    def unpack_cells(packed):
        columns = packed.shape[2] * 5 // 4
        tail = columns // 5
        values = packed[...].reshape(rows, columns - tail)
        inner = lax.rem(lax.broadcasted_iota(jnp.int32, (rows, 1), 0), ROWS)
        keep = jnp.where(inner < frames * cells // SHARDS, 1.0, 0.0)
        main = values.astype(high) * keep
        last = sum(nn_dot(tail_map[f], values[:, f * tail : (f + 1) * tail]) for f in range(frames))
        return jnp.concatenate([main, last], axis=1).astype(low)

    def norm_rows():
        values = tok[...].reshape(count, width).astype(high)
        centered = values - jnp.mean(values, axis=-1, keepdims=True)
        inverse = lax.rsqrt(jnp.mean(centered * centered, axis=-1, keepdims=True) + NORM_EPS)
        return (centered * inverse, inverse)

    gains = gain[...].reshape(1, width)
    pack_frames((norm_rows()[0] * gains).astype(low), norm_s)
    send_peers(norm_s, norm_r, no_send, no_recv)

    def from_column(i):
        mine = lax.rem(z + 4 - i, 4) * 4 + plane
        wait_item(mine)
        pass_item(mine, xn, 3 + i).start()
        pass_item(mine, yn, 7 + i).start()
        pair_item(mine).start()

    def from_plane(i):
        level = lax.rem(z + 4 - i, 4) * 4
        from_x = level + lax.rem(xn, 4)
        from_y = level + lax.rem(yn, 4)
        wait_item(from_x)

        @pl.when(c == 0)
        def _():
            pass_item(from_x, yn, 11 + i).start()

        pair_item(from_x).start()
        wait_item(from_y)

        @pl.when(c == 1)
        def _():
            pass_item(from_y, xn, 11 + i).start()

        pair_item(from_y).start()

    from_column(1)
    from_plane(0)
    pack_frames(gout[...].reshape(count, width), go_s)
    send_peers(go_s, go_r, go_send, go_recv)
    from_column(2)
    from_column(3)
    for i in range(1, 4):
        from_plane(i)
    for i in range(4):
        across = lax.rem(z + 4 - i, 4) * 4 + 3 - plane
        wait_item(across)
        pair_item(across).start()

    wait_peers(norm_s, norm_r, no_send, no_recv, False)
    normed = unpack_cells(norm_r)

    other = pl.ds(2 - 2 * c, 2)

    @pl.loop(1, SHARDS)
    def _(d):
        s = lax.rem(t + d, SHARDS)
        to_pair(
            wall.at[other, s], wall.at[other, s], sib_send.at[s], sib_recv.at[s]
        ).wait_recv()

    def full(j):
        return wall[j].reshape(SHARDS * depth, att)

    def output_half(j):
        blocks = wall[3].astype(high)[:, j * share : (j + 1) * share]
        return blocks.reshape(SHARDS * share, att).astype(low)

    q_s[...] = nn_dot(normed, full(0)).astype(low)
    k_s[...] = nn_dot(normed, full(1)).astype(low)
    v_s[...] = nn_dot(normed, full(2)).astype(low)

    codes = jnp.broadcast_to(code_row[...].astype(high), (rows, rows))
    same = codes == codes.T
    acc_a[...] = jnp.zeros_like(acc_a)
    for head in range(HEADS):
        window, inside = head_window(head, head_dim)
        scores = nt_dot(q_s[:, window] * inside, k_s[:, window]) * scale
        scores = jnp.where(same, scores, -jnp.inf)
        expons = jnp.exp(scores - jnp.max(scores, axis=-1, keepdims=True))
        probs = expons / jnp.sum(expons, axis=-1, keepdims=True)
        probs_s[head] = probs
        acc_a[:, window] += nn_dot(probs.astype(low), v_s[:, window] * inside)
    mix_b[...] = acc_a[...].astype(low)
    pack_cells(mix_b[...], mix_s)
    send_peers(mix_s, mix_r, mi_send, mi_recv)

    wait_peers(go_s, go_r, go_send, go_recv, False)
    grad_b[...] = unpack_cells(go_r)

    for j in range(2):
        term = tn_dot(mix_b[...], grad_b[:, j * att : (j + 1) * att])
        term = term.reshape(4, 4, share, att).astype(low)
        for level in range(4):
            for place in range(4):
                dwp[j, place, level] = term[level, place]
    pair_term = to_pair(dwp.at[1 - c], dw_in, pair_send.at[0], pair_recv.at[0])
    pair_term.start()

    gm_s[...] = (
        nt_dot(grad_b[:, :att], output_half(0)) + nt_dot(grad_b[:, att:], output_half(1))
    ).astype(low)

    pair_term.wait_recv()

    def mate_copy(d):
        mate = lax.rem(plane + d, 4)
        return to_tm(dwa_s.at[mate], dwa_r.at[plane], da_send.at[mate], da_recv.at[plane], z * 4 + mate)

    @pl.loop(0, 4)
    def _(place):
        total = dwp[c, place].astype(high) + dw_in[place].astype(high)
        dwa_s[place] = total.astype(low)

    for d in range(1, 4):
        mate_copy(d).start()
    dwa_r[plane] = dwa_s[plane]

    acc_a[...] = jnp.zeros_like(acc_a)
    acc_b[...] = jnp.zeros_like(acc_b)
    acc_c[...] = jnp.zeros_like(acc_c)
    for head in range(HEADS):
        window, inside = head_window(head, head_dim)
        grad_head = gm_s[:, window] * inside
        probs = probs_s[head]
        grad_probs = nt_dot(grad_head, v_s[:, window])
        centre = jnp.sum(probs * grad_probs, axis=-1, keepdims=True)
        grad_scores = (probs * (grad_probs - centre) * scale).astype(low)
        acc_a[:, window] += nn_dot(grad_scores, k_s[:, window] * inside)
        acc_b[:, window] += tn_dot(grad_scores, q_s[:, window] * inside)
        acc_c[:, window] += tn_dot(probs.astype(low), grad_head)
    total = nt_dot(acc_a[...].astype(low), full(0))
    total += nt_dot(acc_b[...].astype(low), full(1))
    total += nt_dot(acc_c[...].astype(low), full(2))
    pack_cells(total.astype(low), gn_s)
    send_peers(gn_s, gn_r, gn_send, gn_recv)

    def level_copy(d):
        level = lax.rem(z + d, 4)
        return to_tm(dwb_s.at[level], dwb_r.at[z], db_send.at[level], db_recv.at[z], level * 4 + plane)

    for d in range(1, 4):
        mate = lax.rem(plane + d, 4)
        to_tm(dwa_s.at[mate], dwa_r.at[mate], da_send.at[mate], da_recv.at[mate], z * 4 + mate).wait_recv()
    dwb_s[...] = jnp.sum(dwa_r[...].astype(high), axis=0).astype(low)
    for d in range(1, 4):
        level_copy(d).start()
    dwb_r[z] = dwb_s[z]

    wait_peers(mix_s, mix_r, mi_send, mi_recv, False)
    mixed_frames = unpack_frames(mix_r).astype(low)
    for j in range(2):
        columns = slice(j * att, (j + 1) * att)
        update = nn_dot(mixed_frames, output_half(j))
        rows_out = tok[:, :, columns].reshape(count, att).astype(high) + update
        block_o[:, :, columns] = rows_out.astype(low).reshape(frames, cells, att)

    for d in range(1, 4):
        level = lax.rem(z + d, 4)
        to_tm(dwb_s.at[level], dwb_r.at[level], db_send.at[level], db_recv.at[level], level * 4 + plane).wait_recv()
    dwf[c] = jnp.sum(dwb_r[...].astype(high), axis=0)
    pair_sum = to_pair(dwf.at[c], dwf.at[c], pair_send.at[1], pair_recv.at[1])
    pair_sum.start()

    scaled, inverse = norm_rows()
    wait_peers(gn_s, gn_r, gn_send, gn_recv, False)
    weighted = unpack_frames(gn_r) * gains
    first = jnp.mean(weighted, axis=-1, keepdims=True)
    second = jnp.mean(weighted * scaled, axis=-1, keepdims=True)
    result = inverse * (weighted - first - scaled * second)
    result = result + gout[...].reshape(count, width).astype(high)
    gtok_o[...] = result.astype(low).reshape(frames, cells, width)

    to_pair(dwf.at[1 - c], dwf.at[1 - c], pair_send.at[1], pair_recv.at[1]).wait_recv()
    dw_o[:, :att] = dwf[0]
    dw_o[:, att:] = dwf[1]

    pair_term.wait_send()
    pair_sum.wait_send()
    for slot in range(15):
        pass_item(t, xn, slot).wait_send()

    @pl.loop(1, SHARDS)
    def _(d):
        pair_item(lax.rem(t + d, SHARDS)).wait_send()

    for d in range(1, 4):
        mate_copy(d).wait_send()
        level_copy(d).wait_send()
    wait_peers(go_s, go_r, go_send, go_recv, True)
    wait_peers(norm_s, norm_r, no_send, no_recv, True)
    wait_peers(mix_s, mix_r, mi_send, mi_recv, True)
    wait_peers(gn_s, gn_r, gn_send, gn_recv, True)


def on_chip_grid(
    frame_tokens,
    visible,
    grad_output,
    norm_gain,
    query_weight,
    key_weight,
    value_weight,
    output_weight,
):
    tokens = frame_tokens[0]
    frames, cells, width = tokens.shape
    groups = cells // SHARDS
    depth, att = query_weight.shape
    share = output_weight.shape[0]
    local = lax.dynamic_slice_in_dim(visible[0], lax.axis_index("tm") * groups, groups, 1)
    codes = local + 4 * jnp.arange(groups, dtype=jnp.int32)[None]
    codes = jnp.pad(
        codes.reshape(SHARDS, frames * groups),
        ((0, 0), (0, ROWS - frames * groups)),
        constant_values=-1,
    )
    rows = SHARDS * ROWS
    low, high = jnp.bfloat16, jnp.float32
    vmem = pl.BlockSpec(memory_space=pltpu.VMEM)
    dma = pltpu.SemaphoreType.DMA
    wide = pltpu.VMEM((SHARDS, ROWS, width * 4 // 5), low)
    thin = pltpu.VMEM((SHARDS, ROWS, att * 4 // 5), low)
    plain = pltpu.VMEM((rows, att), low)
    total = pltpu.VMEM((rows, att), high)
    quarter = pltpu.VMEM((4, 4, share, att), low)
    block_rows, grad_rows, grad_weight = pl.pallas_call(
        fused_kernel,
        out_shape=(
            jax.ShapeDtypeStruct(tokens.shape, low),
            jax.ShapeDtypeStruct(tokens.shape, low),
            jax.ShapeDtypeStruct((share, width), high),
        ),
        in_specs=[vmem] * 8,
        out_specs=(vmem,) * 3,
        scratch_shapes=[
            pltpu.VMEM((4, SHARDS, depth, att), low),
            pltpu.VMEM((1 + frames, rows, frames * cells), low),
            pltpu.VMEM((frames, rows, rows), low),
            wide, wide, wide, wide,
            pltpu.VMEM((rows, width), low),
            plain, plain, plain, plain,
            pltpu.VMEM((HEADS, rows, rows), high),
            total, total, total,
            plain, thin, thin, wide, wide,
            pltpu.VMEM((2, 4, 4, share, att), low),
            quarter, quarter, quarter,
            pltpu.VMEM((4, share, att), low),
            pltpu.VMEM((4, share, att), low),
            pltpu.VMEM((2, share, att), high),
            dma((15,)),
            *[dma((SHARDS,))] * 11,
            *[dma((4,))] * 4,
            dma((2,)),
            dma((2,)),
        ],
        compiler_params=pltpu.CompilerParams(
            collective_id=0, has_side_effects=True, vmem_limit_bytes=56 * 1024 * 1024
        ),
        name="temporal_block",
    )(
        tokens,
        grad_output[0],
        norm_gain,
        codes.reshape(1, rows),
        query_weight,
        key_weight,
        value_weight,
        output_weight,
    )
    return (block_rows[None], grad_rows[None], grad_weight)


def solution(mesh):
    chip_grid = mesh.shape["tm"] == SHARDS and mesh.shape["dp"] == 2
    return jax.shard_map(
        on_chip_grid if chip_grid else on_device,
        mesh=mesh,
        in_specs=(
            P("dp", "tm", None, None),
            P("dp", None, None),
            P("dp", "tm", None, None),
            P(),
            P("tm", None),
            P("tm", None),
            P("tm", None),
            P("tm", None),
        ),
        out_specs=(P("dp", "tm", None, None), P("dp", "tm", None, None), P("tm", None)),
        check_vma=False,
    )
```

```python
import math

import jax
import jax.numpy as jnp
from jax import lax
from jax.experimental import pallas as pl
from jax.experimental.pallas import tpu as pltpu
from jax.sharding import PartitionSpec as P

HEADS = 8


NORM_EPS = 1e-06


def normalize(token_rows, norm_gain):
    values = token_rows.astype(jnp.float32)
    centered = values - jnp.mean(values, axis=-1, keepdims=True)
    inverse = lax.rsqrt(jnp.mean(centered * centered, axis=-1, keepdims=True) + NORM_EPS)
    scaled = centered * inverse
    return (scaled, inverse, (scaled * norm_gain).astype(jnp.bfloat16))


def project(token_rows, weight):
    lead_shape = token_rows.shape[:-1]
    flat_rows = token_rows.reshape(-1, token_rows.shape[-1])
    result = jnp.dot(flat_rows, weight, preferred_element_type=jnp.float32)
    return result.astype(jnp.bfloat16).reshape(lead_shape + (weight.shape[1],))


def split_heads(values):
    return values.reshape(values.shape[:-1] + (HEADS, values.shape[-1] // HEADS))


def attend(query_rows, key_rows, value_rows, same_cell):
    score_scale = 1.0 / math.sqrt(query_rows.shape[-1] // HEADS)
    query_heads = split_heads(query_rows)
    key_heads = split_heads(key_rows)
    value_heads = split_heads(value_rows)
    scores = (
        jnp.einsum("fghe,tghe->ghft", query_heads, key_heads, preferred_element_type=jnp.float32)
        * score_scale
    )
    scores = jnp.where(same_cell[:, None], scores, -jnp.inf)
    row_top = jnp.max(scores, axis=-1, keepdims=True)
    expons = jnp.exp(scores - row_top)
    soft_probs = expons / jnp.sum(expons, axis=-1, keepdims=True)
    probs_low = soft_probs.astype(jnp.bfloat16)
    mixed_rows = jnp.einsum(
        "ghft,tghe->fghe", probs_low, value_heads, preferred_element_type=jnp.float32
    )
    return (soft_probs, probs_low, mixed_rows.reshape(query_rows.shape).astype(jnp.bfloat16))


def attend_back(query_rows, key_rows, value_rows, soft_probs, probs_low, grad_mixed):
    score_scale = 1.0 / math.sqrt(query_rows.shape[-1] // HEADS)
    query_heads = split_heads(query_rows)
    key_heads = split_heads(key_rows)
    value_heads = split_heads(value_rows)
    grad_heads = split_heads(grad_mixed)
    grad_probs = jnp.einsum(
        "fghe,tghe->ghft", grad_heads, value_heads, preferred_element_type=jnp.float32
    )
    centre = jnp.sum(soft_probs * grad_probs, axis=-1, keepdims=True)
    grad_scores = (soft_probs * (grad_probs - centre) * score_scale).astype(jnp.bfloat16)
    grad_query = jnp.einsum(
        "ghft,tghe->fghe", grad_scores, key_heads, preferred_element_type=jnp.float32
    )
    grad_key = jnp.einsum(
        "ghft,fghe->tghe", grad_scores, query_heads, preferred_element_type=jnp.float32
    )
    grad_value = jnp.einsum(
        "ghft,fghe->tghe", probs_low, grad_heads, preferred_element_type=jnp.float32
    )
    full_shape = query_rows.shape
    return (
        grad_query.reshape(full_shape).astype(jnp.bfloat16),
        grad_key.reshape(full_shape).astype(jnp.bfloat16),
        grad_value.reshape(full_shape).astype(jnp.bfloat16),
    )


def back_project(grad_query, grad_key, grad_value, query_weight, key_weight, value_weight):
    lead_shape = grad_query.shape[:-1]
    width = grad_query.shape[-1]
    total = jnp.dot(
        grad_query.reshape(-1, width), query_weight.T, preferred_element_type=jnp.float32
    )
    total = total + jnp.dot(
        grad_key.reshape(-1, width), key_weight.T, preferred_element_type=jnp.float32
    )
    total = total + jnp.dot(
        grad_value.reshape(-1, width), value_weight.T, preferred_element_type=jnp.float32
    )
    return total.astype(jnp.bfloat16).reshape(lead_shape + (query_weight.shape[0],))


def on_device(
    frame_tokens,
    visible,
    grad_output,
    norm_gain,
    query_weight,
    key_weight,
    value_weight,
    output_weight,
):
    query_weight, key_weight, value_weight, output_weight = (
        lax.all_gather(query_weight, "tm", axis=0, tiled=True),
        lax.all_gather(key_weight, "tm", axis=0, tiled=True),
        lax.all_gather(value_weight, "tm", axis=0, tiled=True),
        lax.all_gather(output_weight, "tm", axis=0, tiled=True),
    )
    shards = lax.axis_size("tm")
    tokens = frame_tokens[0]
    frame_count, visible_count, width = tokens.shape
    att_width = output_weight.shape[0]
    groups = visible_count // shards
    scaled, inverse, normed = normalize(tokens, norm_gain)
    local_cells = lax.dynamic_slice_in_dim(visible[0], lax.axis_index("tm") * groups, groups, 1)
    cell_major = local_cells.T
    same_cell = cell_major[:, :, None] == cell_major[:, None, :]
    query_rows = project(normed, query_weight)
    key_rows = project(normed, key_weight)
    value_rows = project(normed, value_weight)
    query_rows, key_rows, value_rows = (
        lax.all_to_all(query_rows, "tm", split_axis=1, concat_axis=0, tiled=True),
        lax.all_to_all(key_rows, "tm", split_axis=1, concat_axis=0, tiled=True),
        lax.all_to_all(value_rows, "tm", split_axis=1, concat_axis=0, tiled=True),
    )
    soft_probs, probs_low, mixed_cells = attend(query_rows, key_rows, value_rows, same_cell)
    mixed_frames = lax.all_to_all(mixed_cells, "tm", split_axis=0, concat_axis=1, tiled=True)
    flat_mixed = mixed_frames.reshape(-1, att_width)
    flat_tokens = tokens.reshape(-1, width)
    update = jnp.dot(flat_mixed, output_weight, preferred_element_type=jnp.float32)
    block_rows = (
        (flat_tokens.astype(jnp.float32) + update).astype(jnp.bfloat16).reshape(tokens.shape)
    )
    flat_grad = grad_output[0].reshape(-1, width)
    grad_mixed = jnp.dot(flat_grad, output_weight.T, preferred_element_type=jnp.float32)
    grad_mixed = grad_mixed.astype(jnp.bfloat16).reshape(frame_count, visible_count, att_width)
    term_share = lax.psum_scatter(
        jnp.dot(flat_mixed.T, flat_grad, preferred_element_type=jnp.float32),
        "tm",
        scatter_dimension=0,
        tiled=True,
    )
    grad_weight = lax.psum(term_share.astype(jnp.bfloat16), "dp").astype(jnp.float32)
    grad_cells = lax.all_to_all(grad_mixed, "tm", split_axis=1, concat_axis=0, tiled=True)
    grad_query, grad_key, grad_value = attend_back(
        query_rows, key_rows, value_rows, soft_probs, probs_low, grad_cells
    )
    grad_query, grad_key, grad_value = (
        lax.all_to_all(grad_query, "tm", split_axis=0, concat_axis=1, tiled=True),
        lax.all_to_all(grad_key, "tm", split_axis=0, concat_axis=1, tiled=True),
        lax.all_to_all(grad_value, "tm", split_axis=0, concat_axis=1, tiled=True),
    )
    grad_normed = back_project(
        grad_query, grad_key, grad_value, query_weight, key_weight, value_weight
    )
    weighted = grad_normed.astype(jnp.float32) * norm_gain
    first_mean = jnp.mean(weighted, axis=-1, keepdims=True)
    second_mean = jnp.mean(weighted * scaled, axis=-1, keepdims=True)
    grad_rows = inverse * (weighted - first_mean - scaled * second_mean) + grad_output[0].astype(
        jnp.float32
    )
    return (block_rows[None], grad_rows.astype(jnp.bfloat16)[None], grad_weight)


SHARDS = 16
ROWS = 16


def nt_dot(left, right):
    return lax.dot_general(left, right, (((1,), (1,)), ((), ())), preferred_element_type=jnp.float32)


def tn_dot(left, right):
    return lax.dot_general(left, right, (((0,), (0,)), ((), ())), preferred_element_type=jnp.float32)


def nn_dot(left, right):
    return jnp.dot(left, right, preferred_element_type=jnp.float32)


def head_window(head, head_dim):
    low = head * head_dim
    start = low // 128 * 128
    stop = -(-(low + head_dim) // 128) * 128
    lane = lax.broadcasted_iota(jnp.int32, (1, stop - start), 1) + start
    inside = jnp.where((lane >= low) & (lane < low + head_dim), 1.0, 0.0)
    return (slice(start, stop), inside.astype(jnp.bfloat16))


def block_maps(cells, frames, row_map, tail_map):
    groups = cells // SHARDS
    taken = frames * groups
    rows = SHARDS * ROWS
    place = lax.broadcasted_iota(jnp.int32, (rows, frames * cells), 0)
    source = lax.broadcasted_iota(jnp.int32, (rows, frames * cells), 1)
    owner, inner = lax.div(place, ROWS), lax.rem(place, ROWS)
    wanted = lax.div(inner, groups) * cells + owner * groups + lax.rem(inner, groups)
    main = (inner < taken) & (source == wanted)
    row_map[0] = jnp.where(main, 1.0, 0.0).astype(jnp.bfloat16)
    for frame in range(frames):
        tail = (inner >= taken) & (source == frame * cells + owner * groups + inner - taken)
        row_map[1 + frame] = jnp.where(tail, 1.0, 0.0).astype(jnp.bfloat16)
    place = lax.broadcasted_iota(jnp.int32, (rows, rows), 0)
    source = lax.broadcasted_iota(jnp.int32, (rows, rows), 1)
    inner = lax.rem(place, ROWS)
    wanted = place - inner + taken + lax.rem(inner, groups)
    for frame in range(frames):
        hit = (lax.div(inner, groups) == frame) & (source == wanted)
        tail_map[frame] = jnp.where(hit, 1.0, 0.0).astype(jnp.bfloat16)


def fused_kernel(
    tok, gout, gain, code_row, wq, wk, wv, wo,
    block_o, gtok_o, dw_o,
    wall, row_map, tail_map, norm_s, norm_r, q_s, k_s, v_s, gm_s, probs_s,
    acc_a, acc_b, acc_c, gm_out, gm_in, mix_s, mix_r, gn_s, gn_r,
    dwp, dw_in, dwa_s, dwa_r, dwb_s, dwb_r, dwf,
    w_send, w_recv, sib_send, sib_recv, gm_send, gm_recv, no_send, no_recv,
    mi_send, mi_recv, gn_send, gn_recv, da_send, da_recv, db_send, db_recv, pair_send, pair_recv,
):
    t = lax.axis_index("tm")
    c = lax.axis_index("dp")
    x = lax.rem(t, 2)
    y = lax.rem(lax.div(t, 2), 2)
    z = lax.div(t, 4)
    plane = lax.rem(t, 4)
    xn = t + 1 - 2 * x
    yn = t + 2 - 4 * y
    att = q_s.shape[1]
    frames, cells, width = tok.shape
    count = frames * cells
    depth = wq.shape[0]
    share = wo.shape[0]
    rows = SHARDS * ROWS
    head_dim = att // HEADS
    scale = 1.0 / math.sqrt(head_dim)
    low, high = jnp.bfloat16, jnp.float32

    def to_tm(src, dst, send, recv, peer):
        return pltpu.make_async_remote_copy(
            src_ref=src, dst_ref=dst, send_sem=send, recv_sem=recv,
            device_id={"tm": peer}, device_id_type=pl.DeviceIdType.MESH,
        )

    def to_pair(src, dst, send, recv):
        return pltpu.make_async_remote_copy(
            src_ref=src, dst_ref=dst, send_sem=send, recv_sem=recv,
            device_id={"dp": 1 - c}, device_id_type=pl.DeviceIdType.MESH,
        )

    barrier = pltpu.get_barrier_semaphore()

    @pl.loop(1, SHARDS)
    def _(d):
        pl.semaphore_signal(
            barrier, inc=1, device_id={"tm": lax.rem(t + d, SHARDS)},
            device_id_type=pl.DeviceIdType.MESH,
        )

    pl.semaphore_signal(
        barrier, inc=1, device_id={"dp": 1 - c}, device_id_type=pl.DeviceIdType.MESH
    )
    wall[0, t] = wq[...]
    wall[1, t] = wk[...]
    wall[2, t] = wv[...]
    output_rows = wo[...].astype(high)
    wall[3, t] = jnp.concatenate([output_rows[:, :att], output_rows[:, att:]], axis=0).astype(low)
    pl.semaphore_wait(barrier, SHARDS)

    def item(h, s):
        return wall.at[3 * c if h == 0 else 1 + c, s]

    def pass_item(h, s, peer, kind):
        slot = (h * 5 + kind) * 4 + lax.div(s, 4)
        return to_tm(item(h, s), item(h, s), w_send.at[slot], w_recv.at[h * SHARDS + s], peer)

    def wait_item(h, s):
        pass_item(h, s, xn, 0).wait_recv()

    def pair_item(h, s):
        slot = h * SHARDS + s
        return to_pair(item(h, s), item(h, s), sib_send.at[slot], sib_recv.at[slot])

    def go_up(h, s):
        @pl.when(z < 3)
        def _():
            pass_item(h, s, t + 4, 0).start()

    def go_down(h, s):
        @pl.when(z > 0)
        def _():
            pass_item(h, s, t - 4, 1).start()

    def go_across(h, s):
        pass_item(h, s, xn, 2).start()
        pass_item(h, s, yn, 3).start()

    def at_levels(k, action):
        if k == 0:
            action(t, None)
        else:
            @pl.when(z >= k)
            def _():
                action(t - 4 * k, go_up)

            @pl.when(z + k <= 3)
            def _():
                action(t + 4 * k, go_down)

    def from_column(h, k):
        def action(s, onward):
            wait_item(h, s)
            onward(h, s)
            go_across(h, s)
            pair_item(h, s).start()

        at_levels(k, action)

    def from_plane(h, k):
        def action(s, _):
            level = s - plane
            from_x = level + lax.rem(xn, 4)
            from_y = level + lax.rem(yn, 4)
            wait_item(h, from_x)

            @pl.when(c == 0)
            def _():
                pass_item(h, from_x, yn, 4).start()

            pair_item(h, from_x).start()
            wait_item(h, from_y)

            @pl.when(c == 1)
            def _():
                pass_item(h, from_y, xn, 4).start()

            pair_item(h, from_y).start()

        at_levels(k, action)

    def from_across(h):
        for level in range(4):
            across = level * 4 + 3 - plane
            wait_item(h, across)
            pair_item(h, across).start()

    def send_own(h):
        go_up(h, t)
        go_down(h, t)
        go_across(h, t)

    def wait_pair(h):
        @pl.loop(1, SHARDS)
        def _(d):
            s = lax.rem(t + d, SHARDS)
            slot = h * SHARDS + s
            landed = wall.at[3 * (1 - c) if h == 0 else 2 - c, s]
            to_pair(landed, landed, sib_send.at[slot], sib_recv.at[slot]).wait_recv()

    send_own(0)

    def peer_copy(src, dst, send, recv, peer):
        return to_tm(src.at[peer], dst.at[t], send.at[peer], recv.at[t], peer)

    def send_peers(src, dst, send, recv):
        @pl.loop(1, SHARDS)
        def _(d):
            peer_copy(src, dst, send, recv, lax.rem(t + d, SHARDS)).start()

        dst[t] = src[t]

    def wait_peers(src, dst, send, recv, sends):
        @pl.loop(1, SHARDS)
        def _(d):
            peer = lax.rem(t + d, SHARDS)
            if sends:
                peer_copy(src, dst, send, recv, peer).wait_send()
            else:
                to_tm(src.at[peer], dst.at[peer], send.at[peer], recv.at[peer], peer).wait_recv()

    block_maps(cells, frames, row_map, tail_map)

    def pack_frames(values, out):
        columns = values.shape[1]
        tail = columns // 5
        packed = nn_dot(row_map[0], values[:, : columns - tail])
        spare = [nn_dot(row_map[1 + f], values[:, columns - tail :]) for f in range(frames)]
        spare.append(jnp.zeros((rows, columns - tail - frames * tail), high))
        packed = packed + jnp.concatenate(spare, axis=1)
        out[...] = packed.astype(low).reshape(out.shape)

    def pack_cells(values, out):
        columns = values.shape[1]
        tail = columns // 5
        spare = [tn_dot(tail_map[f], values[:, columns - tail :]) for f in range(frames)]
        spare.append(jnp.zeros((rows, columns - tail - frames * tail), high))
        packed = values[:, : columns - tail].astype(high) + jnp.concatenate(spare, axis=1)
        out[...] = packed.astype(low).reshape(out.shape)

    def unpack_frames(packed):
        columns = packed.shape[2] * 5 // 4
        tail = columns // 5
        values = packed[...].reshape(rows, columns - tail)
        main = tn_dot(row_map[0], values)
        last = sum(tn_dot(row_map[1 + f], values[:, f * tail : (f + 1) * tail]) for f in range(frames))
        return jnp.concatenate([main, last], axis=1)

    def unpack_cells(packed):
        columns = packed.shape[2] * 5 // 4
        tail = columns // 5
        values = packed[...].reshape(rows, columns - tail)
        inner = lax.rem(lax.broadcasted_iota(jnp.int32, (rows, 1), 0), ROWS)
        keep = jnp.where(inner < frames * cells // SHARDS, 1.0, 0.0)
        main = values.astype(high) * keep
        last = sum(nn_dot(tail_map[f], values[:, f * tail : (f + 1) * tail]) for f in range(frames))
        return jnp.concatenate([main, last], axis=1).astype(low)

    def norm_rows():
        values = tok[...].reshape(count, width).astype(high)
        centered = values - jnp.mean(values, axis=-1, keepdims=True)
        inverse = lax.rsqrt(jnp.mean(centered * centered, axis=-1, keepdims=True) + NORM_EPS)
        return (centered * inverse, inverse)

    gains = gain[...].reshape(1, width)
    pack_frames((norm_rows()[0] * gains).astype(low), norm_s)
    send_peers(norm_s, norm_r, no_send, no_recv)

    from_column(0, 1)
    send_own(1)
    from_plane(0, 0)
    from_column(0, 2)
    from_column(1, 1)
    from_plane(0, 1)
    from_plane(1, 0)
    from_column(0, 3)
    from_column(1, 2)
    from_plane(0, 2)
    from_plane(1, 1)
    from_column(1, 3)
    from_plane(0, 3)
    from_plane(1, 2)
    from_across(0)
    from_plane(1, 3)
    wait_pair(0)

    def full(j):
        return wall[j].reshape(SHARDS * depth, att)

    def output_half(j):
        blocks = wall[3].astype(high)[:, j * share : (j + 1) * share]
        return blocks.reshape(SHARDS * share, att).astype(low)

    grads = gout[...].reshape(count, width)
    grad_mixed = nt_dot(grads[:, :att], output_half(0)) + nt_dot(grads[:, att:], output_half(1))
    pack_frames(grad_mixed.astype(low), gm_out)
    send_peers(gm_out, gm_in, gm_send, gm_recv)

    from_across(1)
    wait_peers(norm_s, norm_r, no_send, no_recv, False)
    normed = unpack_cells(norm_r)
    q_s[...] = nn_dot(normed, full(0)).astype(low)
    wait_pair(1)
    k_s[...] = nn_dot(normed, full(1)).astype(low)
    v_s[...] = nn_dot(normed, full(2)).astype(low)

    codes = jnp.broadcast_to(code_row[...].astype(high), (rows, rows))
    same = codes == codes.T
    acc_a[...] = jnp.zeros_like(acc_a)
    for head in range(HEADS):
        window, inside = head_window(head, head_dim)
        scores = nt_dot(q_s[:, window] * inside, k_s[:, window]) * scale
        scores = jnp.where(same, scores, -jnp.inf)
        expons = jnp.exp(scores - jnp.max(scores, axis=-1, keepdims=True))
        probs = expons / jnp.sum(expons, axis=-1, keepdims=True)
        probs_s[head] = probs
        acc_a[:, window] += nn_dot(probs.astype(low), v_s[:, window] * inside)
    pack_cells(acc_a[...].astype(low), mix_s)
    send_peers(mix_s, mix_r, mi_send, mi_recv)

    wait_peers(gm_out, gm_in, gm_send, gm_recv, False)
    gm_s[...] = unpack_cells(gm_in)

    acc_a[...] = jnp.zeros_like(acc_a)
    acc_b[...] = jnp.zeros_like(acc_b)
    acc_c[...] = jnp.zeros_like(acc_c)
    for head in range(HEADS):
        window, inside = head_window(head, head_dim)
        grad_head = gm_s[:, window] * inside
        probs = probs_s[head]
        grad_probs = nt_dot(grad_head, v_s[:, window])
        centre = jnp.sum(probs * grad_probs, axis=-1, keepdims=True)
        grad_scores = (probs * (grad_probs - centre) * scale).astype(low)
        acc_a[:, window] += nn_dot(grad_scores, k_s[:, window] * inside)
        acc_b[:, window] += tn_dot(grad_scores, q_s[:, window] * inside)
        acc_c[:, window] += tn_dot(probs.astype(low), grad_head)
    wait_peers(mix_s, mix_r, mi_send, mi_recv, False)
    mixed_frames = unpack_frames(mix_r).astype(low)
    for j in range(2):
        term = tn_dot(mixed_frames, grads[:, j * att : (j + 1) * att])
        term = term.reshape(4, 4, share, att).astype(low)
        for level in range(4):
            for place in range(4):
                dwp[j, place, level] = term[level, place]
    pair_term = to_pair(dwp.at[1 - c], dw_in, pair_send.at[0], pair_recv.at[0])
    pair_term.start()

    total = nt_dot(acc_a[...].astype(low), full(0))
    total += nt_dot(acc_b[...].astype(low), full(1))
    total += nt_dot(acc_c[...].astype(low), full(2))
    pack_cells(total.astype(low), gn_s)
    send_peers(gn_s, gn_r, gn_send, gn_recv)

    def mate_copy(d):
        mate = lax.rem(plane + d, 4)
        return to_tm(dwa_s.at[mate], dwa_r.at[plane], da_send.at[mate], da_recv.at[plane], z * 4 + mate)

    pair_term.wait_recv()

    @pl.loop(0, 4)
    def _(place):
        both = dwp[c, place].astype(high) + dw_in[place].astype(high)
        dwa_s[place] = both.astype(low)

    for d in range(1, 4):
        mate_copy(d).start()
    dwa_r[plane] = dwa_s[plane]

    for j in range(2):
        columns = slice(j * att, (j + 1) * att)
        update = nn_dot(mixed_frames, output_half(j))
        rows_out = tok[:, :, columns].reshape(count, att).astype(high) + update
        block_o[:, :, columns] = rows_out.astype(low).reshape(frames, cells, att)
    scaled, inverse = norm_rows()

    def level_copy(d):
        level = lax.rem(z + d, 4)
        return to_tm(dwb_s.at[level], dwb_r.at[z], db_send.at[level], db_recv.at[z], level * 4 + plane)

    for d in range(1, 4):
        mate = lax.rem(plane + d, 4)
        to_tm(dwa_s.at[mate], dwa_r.at[mate], da_send.at[mate], da_recv.at[mate], z * 4 + mate).wait_recv()
    dwb_s[...] = jnp.sum(dwa_r[...].astype(high), axis=0).astype(low)
    for d in range(1, 4):
        level_copy(d).start()
    dwb_r[z] = dwb_s[z]

    wait_peers(gn_s, gn_r, gn_send, gn_recv, False)
    weighted = unpack_frames(gn_r) * gains
    first = jnp.mean(weighted, axis=-1, keepdims=True)
    second = jnp.mean(weighted * scaled, axis=-1, keepdims=True)
    result = inverse * (weighted - first - scaled * second)
    result = result + gout[...].reshape(count, width).astype(high)
    gtok_o[...] = result.astype(low).reshape(frames, cells, width)

    for d in range(1, 4):
        level = lax.rem(z + d, 4)
        to_tm(dwb_s.at[level], dwb_r.at[level], db_send.at[level], db_recv.at[level], level * 4 + plane).wait_recv()
    dwf[c] = jnp.sum(dwb_r[...].astype(high), axis=0)
    pair_sum = to_pair(dwf.at[c], dwf.at[c], pair_send.at[1], pair_recv.at[1])
    pair_sum.start()

    to_pair(dwf.at[1 - c], dwf.at[1 - c], pair_send.at[1], pair_recv.at[1]).wait_recv()
    dw_o[:, :att] = dwf[0]
    dw_o[:, att:] = dwf[1]

    pair_term.wait_send()
    pair_sum.wait_send()
    for h in range(2):
        pass_item(h, t, xn, 2).wait_send()
        pass_item(h, t, yn, 3).wait_send()
        for level in range(4):
            @pl.when((z < 3) & (level <= z))
            def _():
                pass_item(h, level * 4 + plane, xn, 0).wait_send()

            @pl.when((z > 0) & (level >= z))
            def _():
                pass_item(h, level * 4 + plane, xn, 1).wait_send()

            @pl.when(level != z)
            def _():
                pass_item(h, level * 4 + plane, xn, 2).wait_send()
                pass_item(h, level * 4 + plane, yn, 3).wait_send()

            pass_item(h, level * 4 + plane, xn, 4).wait_send()

        @pl.loop(1, SHARDS)
        def _(d):
            pair_item(h, lax.rem(t + d, SHARDS)).wait_send()

    for d in range(1, 4):
        mate_copy(d).wait_send()
        level_copy(d).wait_send()
    wait_peers(gm_out, gm_in, gm_send, gm_recv, True)
    wait_peers(norm_s, norm_r, no_send, no_recv, True)
    wait_peers(mix_s, mix_r, mi_send, mi_recv, True)
    wait_peers(gn_s, gn_r, gn_send, gn_recv, True)


def on_chip_grid(
    frame_tokens,
    visible,
    grad_output,
    norm_gain,
    query_weight,
    key_weight,
    value_weight,
    output_weight,
):
    tokens = frame_tokens[0]
    frames, cells, width = tokens.shape
    groups = cells // SHARDS
    depth, att = query_weight.shape
    share = output_weight.shape[0]
    local = lax.dynamic_slice_in_dim(visible[0], lax.axis_index("tm") * groups, groups, 1)
    codes = local + 4 * jnp.arange(groups, dtype=jnp.int32)[None]
    codes = jnp.pad(
        codes.reshape(SHARDS, frames * groups),
        ((0, 0), (0, ROWS - frames * groups)),
        constant_values=-1,
    )
    rows = SHARDS * ROWS
    low, high = jnp.bfloat16, jnp.float32
    vmem = pl.BlockSpec(memory_space=pltpu.VMEM)
    dma = pltpu.SemaphoreType.DMA
    wide = pltpu.VMEM((SHARDS, ROWS, width * 4 // 5), low)
    thin = pltpu.VMEM((SHARDS, ROWS, att * 4 // 5), low)
    plain = pltpu.VMEM((rows, att), low)
    total = pltpu.VMEM((rows, att), high)
    quarter = pltpu.VMEM((4, 4, share, att), low)
    block_rows, grad_rows, grad_weight = pl.pallas_call(
        fused_kernel,
        out_shape=(
            jax.ShapeDtypeStruct(tokens.shape, low),
            jax.ShapeDtypeStruct(tokens.shape, low),
            jax.ShapeDtypeStruct((share, width), high),
        ),
        in_specs=[vmem] * 8,
        out_specs=(vmem,) * 3,
        scratch_shapes=[
            pltpu.VMEM((4, SHARDS, depth, att), low),
            pltpu.VMEM((1 + frames, rows, frames * cells), low),
            pltpu.VMEM((frames, rows, rows), low),
            wide, wide,
            plain, plain, plain, plain,
            pltpu.VMEM((HEADS, rows, rows), high),
            total, total, total,
            thin, thin, thin, thin, wide, wide,
            pltpu.VMEM((2, 4, 4, share, att), low),
            quarter, quarter, quarter,
            pltpu.VMEM((4, share, att), low),
            pltpu.VMEM((4, share, att), low),
            pltpu.VMEM((2, share, att), high),
            dma((40,)),
            *[dma((2 * SHARDS,))] * 3,
            *[dma((SHARDS,))] * 8,
            *[dma((4,))] * 4,
            dma((2,)),
            dma((2,)),
        ],
        compiler_params=pltpu.CompilerParams(
            collective_id=0, has_side_effects=True, vmem_limit_bytes=56 * 1024 * 1024
        ),
        name="temporal_block",
    )(
        tokens,
        grad_output[0],
        norm_gain,
        codes.reshape(1, rows),
        query_weight,
        key_weight,
        value_weight,
        output_weight,
    )
    return (block_rows[None], grad_rows[None], grad_weight)


def solution(mesh):
    chip_grid = mesh.shape["tm"] == SHARDS and mesh.shape["dp"] == 2
    return jax.shard_map(
        on_chip_grid if chip_grid else on_device,
        mesh=mesh,
        in_specs=(
            P("dp", "tm", None, None),
            P("dp", None, None),
            P("dp", "tm", None, None),
            P(),
            P("tm", None),
            P("tm", None),
            P("tm", None),
            P("tm", None),
        ),
        out_specs=(P("dp", "tm", None, None), P("dp", "tm", None, None), P("tm", None)),
        check_vma=False,
    )
```

```python
import math

import jax
import jax.numpy as jnp
from jax import lax
from jax.experimental import pallas as pl
from jax.experimental.pallas import tpu as pltpu
from jax.sharding import PartitionSpec as P

HEADS = 8


NORM_EPS = 1e-06


def normalize(token_rows, norm_gain):
    values = token_rows.astype(jnp.float32)
    centered = values - jnp.mean(values, axis=-1, keepdims=True)
    inverse = lax.rsqrt(jnp.mean(centered * centered, axis=-1, keepdims=True) + NORM_EPS)
    scaled = centered * inverse
    return (scaled, inverse, (scaled * norm_gain).astype(jnp.bfloat16))


def project(token_rows, weight):
    lead_shape = token_rows.shape[:-1]
    flat_rows = token_rows.reshape(-1, token_rows.shape[-1])
    result = jnp.dot(flat_rows, weight, preferred_element_type=jnp.float32)
    return result.astype(jnp.bfloat16).reshape(lead_shape + (weight.shape[1],))


def split_heads(values):
    return values.reshape(values.shape[:-1] + (HEADS, values.shape[-1] // HEADS))


def attend(query_rows, key_rows, value_rows, same_cell):
    score_scale = 1.0 / math.sqrt(query_rows.shape[-1] // HEADS)
    query_heads = split_heads(query_rows)
    key_heads = split_heads(key_rows)
    value_heads = split_heads(value_rows)
    scores = (
        jnp.einsum("fghe,tghe->ghft", query_heads, key_heads, preferred_element_type=jnp.float32)
        * score_scale
    )
    scores = jnp.where(same_cell[:, None], scores, -jnp.inf)
    row_top = jnp.max(scores, axis=-1, keepdims=True)
    expons = jnp.exp(scores - row_top)
    soft_probs = expons / jnp.sum(expons, axis=-1, keepdims=True)
    probs_low = soft_probs.astype(jnp.bfloat16)
    mixed_rows = jnp.einsum(
        "ghft,tghe->fghe", probs_low, value_heads, preferred_element_type=jnp.float32
    )
    return (soft_probs, probs_low, mixed_rows.reshape(query_rows.shape).astype(jnp.bfloat16))


def attend_back(query_rows, key_rows, value_rows, soft_probs, probs_low, grad_mixed):
    score_scale = 1.0 / math.sqrt(query_rows.shape[-1] // HEADS)
    query_heads = split_heads(query_rows)
    key_heads = split_heads(key_rows)
    value_heads = split_heads(value_rows)
    grad_heads = split_heads(grad_mixed)
    grad_probs = jnp.einsum(
        "fghe,tghe->ghft", grad_heads, value_heads, preferred_element_type=jnp.float32
    )
    centre = jnp.sum(soft_probs * grad_probs, axis=-1, keepdims=True)
    grad_scores = (soft_probs * (grad_probs - centre) * score_scale).astype(jnp.bfloat16)
    grad_query = jnp.einsum(
        "ghft,tghe->fghe", grad_scores, key_heads, preferred_element_type=jnp.float32
    )
    grad_key = jnp.einsum(
        "ghft,fghe->tghe", grad_scores, query_heads, preferred_element_type=jnp.float32
    )
    grad_value = jnp.einsum(
        "ghft,fghe->tghe", probs_low, grad_heads, preferred_element_type=jnp.float32
    )
    full_shape = query_rows.shape
    return (
        grad_query.reshape(full_shape).astype(jnp.bfloat16),
        grad_key.reshape(full_shape).astype(jnp.bfloat16),
        grad_value.reshape(full_shape).astype(jnp.bfloat16),
    )


def back_project(grad_query, grad_key, grad_value, query_weight, key_weight, value_weight):
    lead_shape = grad_query.shape[:-1]
    width = grad_query.shape[-1]
    total = jnp.dot(
        grad_query.reshape(-1, width), query_weight.T, preferred_element_type=jnp.float32
    )
    total = total + jnp.dot(
        grad_key.reshape(-1, width), key_weight.T, preferred_element_type=jnp.float32
    )
    total = total + jnp.dot(
        grad_value.reshape(-1, width), value_weight.T, preferred_element_type=jnp.float32
    )
    return total.astype(jnp.bfloat16).reshape(lead_shape + (query_weight.shape[0],))


def on_device(
    frame_tokens,
    visible,
    grad_output,
    norm_gain,
    query_weight,
    key_weight,
    value_weight,
    output_weight,
):
    query_weight, key_weight, value_weight, output_weight = (
        lax.all_gather(query_weight, "tm", axis=0, tiled=True),
        lax.all_gather(key_weight, "tm", axis=0, tiled=True),
        lax.all_gather(value_weight, "tm", axis=0, tiled=True),
        lax.all_gather(output_weight, "tm", axis=0, tiled=True),
    )
    shards = lax.axis_size("tm")
    tokens = frame_tokens[0]
    frame_count, visible_count, width = tokens.shape
    att_width = output_weight.shape[0]
    groups = visible_count // shards
    scaled, inverse, normed = normalize(tokens, norm_gain)
    local_cells = lax.dynamic_slice_in_dim(visible[0], lax.axis_index("tm") * groups, groups, 1)
    cell_major = local_cells.T
    same_cell = cell_major[:, :, None] == cell_major[:, None, :]
    query_rows = project(normed, query_weight)
    key_rows = project(normed, key_weight)
    value_rows = project(normed, value_weight)
    query_rows, key_rows, value_rows = (
        lax.all_to_all(query_rows, "tm", split_axis=1, concat_axis=0, tiled=True),
        lax.all_to_all(key_rows, "tm", split_axis=1, concat_axis=0, tiled=True),
        lax.all_to_all(value_rows, "tm", split_axis=1, concat_axis=0, tiled=True),
    )
    soft_probs, probs_low, mixed_cells = attend(query_rows, key_rows, value_rows, same_cell)
    mixed_frames = lax.all_to_all(mixed_cells, "tm", split_axis=0, concat_axis=1, tiled=True)
    flat_mixed = mixed_frames.reshape(-1, att_width)
    flat_tokens = tokens.reshape(-1, width)
    update = jnp.dot(flat_mixed, output_weight, preferred_element_type=jnp.float32)
    block_rows = (
        (flat_tokens.astype(jnp.float32) + update).astype(jnp.bfloat16).reshape(tokens.shape)
    )
    flat_grad = grad_output[0].reshape(-1, width)
    grad_mixed = jnp.dot(flat_grad, output_weight.T, preferred_element_type=jnp.float32)
    grad_mixed = grad_mixed.astype(jnp.bfloat16).reshape(frame_count, visible_count, att_width)
    term_share = lax.psum_scatter(
        jnp.dot(flat_mixed.T, flat_grad, preferred_element_type=jnp.float32),
        "tm",
        scatter_dimension=0,
        tiled=True,
    )
    grad_weight = lax.psum(term_share.astype(jnp.bfloat16), "dp").astype(jnp.float32)
    grad_cells = lax.all_to_all(grad_mixed, "tm", split_axis=1, concat_axis=0, tiled=True)
    grad_query, grad_key, grad_value = attend_back(
        query_rows, key_rows, value_rows, soft_probs, probs_low, grad_cells
    )
    grad_query, grad_key, grad_value = (
        lax.all_to_all(grad_query, "tm", split_axis=0, concat_axis=1, tiled=True),
        lax.all_to_all(grad_key, "tm", split_axis=0, concat_axis=1, tiled=True),
        lax.all_to_all(grad_value, "tm", split_axis=0, concat_axis=1, tiled=True),
    )
    grad_normed = back_project(
        grad_query, grad_key, grad_value, query_weight, key_weight, value_weight
    )
    weighted = grad_normed.astype(jnp.float32) * norm_gain
    first_mean = jnp.mean(weighted, axis=-1, keepdims=True)
    second_mean = jnp.mean(weighted * scaled, axis=-1, keepdims=True)
    grad_rows = inverse * (weighted - first_mean - scaled * second_mean) + grad_output[0].astype(
        jnp.float32
    )
    return (block_rows[None], grad_rows.astype(jnp.bfloat16)[None], grad_weight)


SHARDS = 16
ROWS = 16


def nt_dot(left, right):
    return lax.dot_general(left, right, (((1,), (1,)), ((), ())), preferred_element_type=jnp.float32)


def tn_dot(left, right):
    return lax.dot_general(left, right, (((0,), (0,)), ((), ())), preferred_element_type=jnp.float32)


def nn_dot(left, right):
    return jnp.dot(left, right, preferred_element_type=jnp.float32)


def head_window(head, head_dim):
    low = head * head_dim
    start = low // 128 * 128
    stop = -(-(low + head_dim) // 128) * 128
    lane = lax.broadcasted_iota(jnp.int32, (1, stop - start), 1) + start
    inside = jnp.where((lane >= low) & (lane < low + head_dim), 1.0, 0.0)
    return (slice(start, stop), inside.astype(jnp.bfloat16))


def block_maps(cells, frames, row_map, tail_map):
    groups = cells // SHARDS
    taken = frames * groups
    rows = SHARDS * ROWS
    place = lax.broadcasted_iota(jnp.int32, (rows, frames * cells), 0)
    source = lax.broadcasted_iota(jnp.int32, (rows, frames * cells), 1)
    owner, inner = lax.div(place, ROWS), lax.rem(place, ROWS)
    wanted = lax.div(inner, groups) * cells + owner * groups + lax.rem(inner, groups)
    main = (inner < taken) & (source == wanted)
    row_map[0] = jnp.where(main, 1.0, 0.0).astype(jnp.bfloat16)
    for frame in range(frames):
        tail = (inner >= taken) & (source == frame * cells + owner * groups + inner - taken)
        row_map[1 + frame] = jnp.where(tail, 1.0, 0.0).astype(jnp.bfloat16)
    place = lax.broadcasted_iota(jnp.int32, (rows, rows), 0)
    source = lax.broadcasted_iota(jnp.int32, (rows, rows), 1)
    inner = lax.rem(place, ROWS)
    wanted = place - inner + taken + lax.rem(inner, groups)
    for frame in range(frames):
        hit = (lax.div(inner, groups) == frame) & (source == wanted)
        tail_map[frame] = jnp.where(hit, 1.0, 0.0).astype(jnp.bfloat16)


def fused_kernel(
    tok, gout, gain, code_row, wq, wk, wv, wo,
    block_o, gtok_o, dw_o,
    wall, row_map, tail_map, norm_s, norm_r, q_s, k_s, v_s, gm_s, probs_s,
    acc_a, acc_b, acc_c, gm_out, gm_in, mix_s, mix_r, gn_s, gn_r,
    dwp, dw_in, dwa_s, dwa_r, dwb_s, dwb_r, dwf,
    w_send, w_recv, sib_send, sib_recv, gm_send, gm_recv, no_send, no_recv,
    mi_send, mi_recv, gn_send, gn_recv, da_send, da_recv, db_send, db_recv, pair_send, pair_recv,
):
    t = lax.axis_index("tm")
    c = lax.axis_index("dp")
    x = lax.rem(t, 2)
    y = lax.rem(lax.div(t, 2), 2)
    z = lax.div(t, 4)
    plane = lax.rem(t, 4)
    xn = t + 1 - 2 * x
    yn = t + 2 - 4 * y
    att = q_s.shape[1]
    frames, cells, width = tok.shape
    count = frames * cells
    depth = wq.shape[0]
    share = wo.shape[0]
    rows = SHARDS * ROWS
    head_dim = att // HEADS
    scale = 1.0 / math.sqrt(head_dim)
    low, high = jnp.bfloat16, jnp.float32

    def to_tm(src, dst, send, recv, peer):
        return pltpu.make_async_remote_copy(
            src_ref=src, dst_ref=dst, send_sem=send, recv_sem=recv,
            device_id={"tm": peer}, device_id_type=pl.DeviceIdType.MESH,
        )

    def to_pair(src, dst, send, recv):
        return pltpu.make_async_remote_copy(
            src_ref=src, dst_ref=dst, send_sem=send, recv_sem=recv,
            device_id={"dp": 1 - c}, device_id_type=pl.DeviceIdType.MESH,
        )

    barrier = pltpu.get_barrier_semaphore()

    @pl.loop(1, SHARDS)
    def _(d):
        pl.semaphore_signal(
            barrier, inc=1, device_id={"tm": lax.rem(t + d, SHARDS)},
            device_id_type=pl.DeviceIdType.MESH,
        )

    pl.semaphore_signal(
        barrier, inc=1, device_id={"dp": 1 - c}, device_id_type=pl.DeviceIdType.MESH
    )
    wall[0, t] = wq[...]
    wall[1, t] = wk[...]
    wall[2, t] = wv[...]
    output_rows = wo[...].astype(high)
    wall[3, t] = jnp.concatenate([output_rows[:, :att], output_rows[:, att:]], axis=0).astype(low)
    pl.semaphore_wait(barrier, SHARDS)

    def item(h, s):
        return wall.at[3 * c if h == 0 else 1 + c, s]

    def pass_item(h, s, peer, kind):
        slot = (h * 5 + kind) * 4 + lax.div(s, 4)
        return to_tm(item(h, s), item(h, s), w_send.at[slot], w_recv.at[h * SHARDS + s], peer)

    def wait_item(h, s):
        pass_item(h, s, xn, 0).wait_recv()

    def pair_item(h, s):
        slot = h * SHARDS + s
        return to_pair(item(h, s), item(h, s), sib_send.at[slot], sib_recv.at[slot])

    def go_up(h, s):
        @pl.when(z < 3)
        def _():
            pass_item(h, s, t + 4, 0).start()

    def go_down(h, s):
        @pl.when(z > 0)
        def _():
            pass_item(h, s, t - 4, 1).start()

    def go_across(h, s):
        pass_item(h, s, xn, 2).start()
        pass_item(h, s, yn, 3).start()

    def at_levels(k, action):
        if k == 0:
            action(t, None)
        else:
            @pl.when(z >= k)
            def _():
                action(t - 4 * k, go_up)

            @pl.when(z + k <= 3)
            def _():
                action(t + 4 * k, go_down)

    def from_column(h, k):
        def action(s, onward):
            wait_item(h, s)
            onward(h, s)
            go_across(h, s)

        at_levels(k, action)

    def from_plane(h, k):
        def action(s, _):
            level = s - plane
            from_x = level + lax.rem(xn, 4)
            from_y = level + lax.rem(yn, 4)
            wait_item(h, from_x)

            @pl.when(c == 0)
            def _():
                pass_item(h, from_x, yn, 4).start()

            wait_item(h, from_y)

            @pl.when(c == 1)
            def _():
                pass_item(h, from_y, xn, 4).start()


        at_levels(k, action)

    def pair_level(h, level):
        return to_pair(
            level_items(c, h, level), level_items(c, h, level),
            sib_send.at[h * SHARDS + level], sib_recv.at[h * SHARDS + level],
        )

    def level_items(core, h, level):
        return wall.at[3 * core if h == 0 else 1 + core, pl.ds(level, 4)]

    def from_across(h, k):
        def action(s, _):
            level = s - plane
            wait_item(h, level + 3 - plane)
            if k == 0:
                for d in range(1, 4):
                    pair_item(h, level + lax.rem(plane + d, 4)).start()
            else:
                pair_level(h, level).start()

        at_levels(k, action)

    def send_own(h):
        go_up(h, t)
        go_down(h, t)
        go_across(h, t)

    def wait_pair(h):
        def action(s, _):
            level = s - plane
            if s is t:
                for d in range(1, 4):
                    mate = level + lax.rem(plane + d, 4)
                    slot = h * SHARDS + mate
                    landed = wall.at[3 * (1 - c) if h == 0 else 2 - c, mate]
                    to_pair(landed, landed, sib_send.at[slot], sib_recv.at[slot]).wait_recv()
            else:
                slot = h * SHARDS + level
                landed = level_items(1 - c, h, level)
                to_pair(landed, landed, sib_send.at[slot], sib_recv.at[slot]).wait_recv()

        for k in range(4):
            at_levels(k, action)

    send_own(0)

    def send_peers(src, dst, send, recv):
        @pl.loop(1, SHARDS)
        def _(d):
            peer = lax.rem(t + d, SHARDS)
            to_tm(src.at[peer], dst.at[t], send.at[0], recv.at[0], peer).start()

        dst[t] = src[t]

    def wait_peers(src, dst, send, recv, sends):
        others = pl.ds(0, SHARDS - 1)
        copies = to_tm(src.at[others], dst.at[others], send.at[0], recv.at[0], xn)
        if sends:
            copies.wait_send()
        else:
            copies.wait_recv()

    block_maps(cells, frames, row_map, tail_map)

    def pack_frames(values, out):
        columns = values.shape[1]
        tail = columns // 5
        packed = nn_dot(row_map[0], values[:, : columns - tail])
        spare = [nn_dot(row_map[1 + f], values[:, columns - tail :]) for f in range(frames)]
        spare.append(jnp.zeros((rows, columns - tail - frames * tail), high))
        packed = packed + jnp.concatenate(spare, axis=1)
        out[...] = packed.astype(low).reshape(out.shape)

    def pack_cells(values, out):
        columns = values.shape[1]
        tail = columns // 5
        spare = [tn_dot(tail_map[f], values[:, columns - tail :]) for f in range(frames)]
        spare.append(jnp.zeros((rows, columns - tail - frames * tail), high))
        packed = values[:, : columns - tail].astype(high) + jnp.concatenate(spare, axis=1)
        out[...] = packed.astype(low).reshape(out.shape)

    def unpack_frames(packed):
        columns = packed.shape[2] * 5 // 4
        tail = columns // 5
        values = packed[...].reshape(rows, columns - tail)
        main = tn_dot(row_map[0], values)
        last = sum(tn_dot(row_map[1 + f], values[:, f * tail : (f + 1) * tail]) for f in range(frames))
        return jnp.concatenate([main, last], axis=1)

    def unpack_cells(packed):
        columns = packed.shape[2] * 5 // 4
        tail = columns // 5
        values = packed[...].reshape(rows, columns - tail)
        inner = lax.rem(lax.broadcasted_iota(jnp.int32, (rows, 1), 0), ROWS)
        keep = jnp.where(inner < frames * cells // SHARDS, 1.0, 0.0)
        main = values.astype(high) * keep
        last = sum(nn_dot(tail_map[f], values[:, f * tail : (f + 1) * tail]) for f in range(frames))
        return jnp.concatenate([main, last], axis=1).astype(low)

    def norm_rows():
        values = tok[...].reshape(count, width).astype(high)
        centered = values - jnp.mean(values, axis=-1, keepdims=True)
        inverse = lax.rsqrt(jnp.mean(centered * centered, axis=-1, keepdims=True) + NORM_EPS)
        return (centered * inverse, inverse)

    gains = gain[...].reshape(1, width)
    pack_frames((norm_rows()[0] * gains).astype(low), norm_s)
    send_peers(norm_s, norm_r, no_send, no_recv)

    from_column(0, 1)
    send_own(1)
    from_plane(0, 0)
    from_column(0, 2)
    from_column(1, 1)
    from_plane(0, 1)
    from_plane(1, 0)
    from_across(0, 0)
    from_column(0, 3)
    from_column(1, 2)
    from_plane(0, 2)
    from_plane(1, 1)
    from_across(0, 1)
    from_across(1, 0)
    from_column(1, 3)
    from_plane(0, 3)
    from_plane(1, 2)
    from_across(0, 2)
    from_across(1, 1)
    from_plane(1, 3)
    from_across(0, 3)
    wait_pair(0)

    def full(j):
        return wall[j].reshape(SHARDS * depth, att)

    def output_half(j):
        blocks = wall[3].astype(high)[:, j * share : (j + 1) * share]
        return blocks.reshape(SHARDS * share, att).astype(low)

    grads = gout[...].reshape(count, width)
    grad_mixed = nt_dot(grads[:, :att], output_half(0)) + nt_dot(grads[:, att:], output_half(1))
    pack_frames(grad_mixed.astype(low), gm_out)
    send_peers(gm_out, gm_in, gm_send, gm_recv)

    from_across(1, 2)
    from_across(1, 3)
    wait_peers(norm_s, norm_r, no_send, no_recv, False)
    normed = unpack_cells(norm_r)
    q_s[...] = nn_dot(normed, full(0)).astype(low)
    wait_pair(1)
    k_s[...] = nn_dot(normed, full(1)).astype(low)
    v_s[...] = nn_dot(normed, full(2)).astype(low)

    codes = jnp.broadcast_to(code_row[...].astype(high), (rows, rows))
    same = codes == codes.T
    acc_a[...] = jnp.zeros_like(acc_a)
    for head in range(HEADS):
        window, inside = head_window(head, head_dim)
        scores = nt_dot(q_s[:, window] * inside, k_s[:, window]) * scale
        scores = jnp.where(same, scores, -jnp.inf)
        expons = jnp.exp(scores - jnp.max(scores, axis=-1, keepdims=True))
        probs = expons * (1.0 / jnp.sum(expons, axis=-1, keepdims=True))
        probs_s[head] = probs
        acc_a[:, window] += nn_dot(probs.astype(low), v_s[:, window] * inside)
    pack_cells(acc_a[...].astype(low), mix_s)
    send_peers(mix_s, mix_r, mi_send, mi_recv)

    wait_peers(gm_out, gm_in, gm_send, gm_recv, False)
    gm_s[...] = unpack_cells(gm_in)

    acc_a[...] = jnp.zeros_like(acc_a)
    acc_b[...] = jnp.zeros_like(acc_b)
    acc_c[...] = jnp.zeros_like(acc_c)
    def back_head(head):
        window, inside = head_window(head, head_dim)
        grad_head = gm_s[:, window] * inside
        probs = probs_s[head]
        grad_probs = nt_dot(grad_head, v_s[:, window])
        centre = jnp.sum(probs * grad_probs, axis=-1, keepdims=True)
        grad_scores = (probs * (grad_probs - centre) * scale).astype(low)
        acc_a[:, window] += nn_dot(grad_scores, k_s[:, window] * inside)
        acc_b[:, window] += tn_dot(grad_scores, q_s[:, window] * inside)
        acc_c[:, window] += tn_dot(probs.astype(low), grad_head)

    for head in range(HEADS // 2):
        back_head(head)

    wait_peers(mix_s, mix_r, mi_send, mi_recv, False)
    mixed_frames = unpack_frames(mix_r).astype(low)
    for j in range(2):
        term = tn_dot(mixed_frames, grads[:, j * att : (j + 1) * att])
        term = term.reshape(4, 4, share, att).astype(low)
        for level in range(4):
            for place in range(4):
                dwp[j, place, level] = term[level, place]
    pair_term = to_pair(dwp.at[1 - c], dw_in, pair_send.at[0], pair_recv.at[0])
    pair_term.start()

    for head in range(HEADS // 2, HEADS):
        back_head(head)

    def mate_copy(d):
        mate = lax.rem(plane + d, 4)
        return to_tm(dwa_s.at[mate], dwa_r.at[plane], da_send.at[mate], da_recv.at[plane], z * 4 + mate)

    pair_term.wait_recv()

    @pl.loop(0, 4)
    def _(place):
        both = dwp[c, place].astype(high) + dw_in[place].astype(high)
        dwa_s[place] = both.astype(low)

    for d in range(1, 4):
        mate_copy(d).start()
    dwa_r[plane] = dwa_s[plane]

    grad_rows = [acc[...].astype(low) for acc in (acc_a, acc_b, acc_c)]
    for j in range(2):
        shards = slice(j * SHARDS // 2, (j + 1) * SHARDS // 2)
        total = sum(
            nt_dot(grad_rows[i], wall[i, shards].reshape(SHARDS // 2 * depth, att)) for i in range(3)
        )
        pack_cells(total.astype(low), gn_s.at[j])
        send_peers(gn_s.at[j], gn_r.at[j], gn_send.at[pl.ds(j, 1)], gn_recv.at[pl.ds(j, 1)])

    for j in range(2):
        columns = slice(j * att, (j + 1) * att)
        update = nn_dot(mixed_frames, output_half(j))
        rows_out = tok[:, :, columns].reshape(count, att).astype(high) + update
        block_o[:, :, columns] = rows_out.astype(low).reshape(frames, cells, att)
    scaled, inverse = norm_rows()

    def finish_items(h):
        pass_item(h, t, xn, 2).wait_send()
        pass_item(h, t, yn, 3).wait_send()
        for level in range(4):
            @pl.when((z < 3) & (level <= z))
            def _():
                pass_item(h, level * 4 + plane, xn, 0).wait_send()

            @pl.when((z > 0) & (level >= z))
            def _():
                pass_item(h, level * 4 + plane, xn, 1).wait_send()

            @pl.when(level != z)
            def _():
                pass_item(h, level * 4 + plane, xn, 2).wait_send()
                pass_item(h, level * 4 + plane, yn, 3).wait_send()
                pair_level(h, level * 4).wait_send()

            pass_item(h, level * 4 + plane, xn, 4).wait_send()
        for d in range(1, 4):
            pair_item(h, z * 4 + lax.rem(plane + d, 4)).wait_send()

    def level_copy(d):
        level = lax.rem(z + d, 4)
        return to_tm(dwb_s.at[level], dwb_r.at[z], db_send.at[level], db_recv.at[z], level * 4 + plane)

    for d in range(1, 4):
        mate = lax.rem(plane + d, 4)
        to_tm(dwa_s.at[mate], dwa_r.at[mate], da_send.at[mate], da_recv.at[mate], z * 4 + mate).wait_recv()
    dwb_s[...] = jnp.sum(dwa_r[...].astype(high), axis=0).astype(low)
    for d in range(1, 4):
        level_copy(d).start()
    dwb_r[z] = dwb_s[z]

    pair_term.wait_send()
    for h in range(2):
        finish_items(h)
    for d in range(1, 4):
        mate_copy(d).wait_send()
    wait_peers(gm_out, gm_in, gm_send, gm_recv, True)
    wait_peers(norm_s, norm_r, no_send, no_recv, True)
    wait_peers(mix_s, mix_r, mi_send, mi_recv, True)

    grad_parts = []
    for j in range(2):
        sems = (gn_send.at[pl.ds(j, 1)], gn_recv.at[pl.ds(j, 1)])
        wait_peers(gn_s.at[j], gn_r.at[j], *sems, False)
        grad_parts.append(unpack_frames(gn_r.at[j]))
    weighted = jnp.concatenate(grad_parts, axis=1) * gains
    first = jnp.mean(weighted, axis=-1, keepdims=True)
    second = jnp.mean(weighted * scaled, axis=-1, keepdims=True)
    result = inverse * (weighted - first - scaled * second)
    result = result + gout[...].reshape(count, width).astype(high)
    gtok_o[...] = result.astype(low).reshape(frames, cells, width)

    for d in range(1, 4):
        level = lax.rem(z + d, 4)
        to_tm(dwb_s.at[level], dwb_r.at[level], db_send.at[level], db_recv.at[level], level * 4 + plane).wait_recv()
    dwf[c] = jnp.sum(dwb_r[...].astype(high), axis=0)
    pair_sum = to_pair(dwf.at[c], dwf.at[c], pair_send.at[1], pair_recv.at[1])
    pair_sum.start()

    to_pair(dwf.at[1 - c], dwf.at[1 - c], pair_send.at[1], pair_recv.at[1]).wait_recv()
    dw_o[:, :att] = dwf[0]
    dw_o[:, att:] = dwf[1]

    pair_sum.wait_send()
    for d in range(1, 4):
        level_copy(d).wait_send()
    for j in range(2):
        sems = (gn_send.at[pl.ds(j, 1)], gn_recv.at[pl.ds(j, 1)])
        wait_peers(gn_s.at[j], gn_r.at[j], *sems, True)


def copy_kernel(*refs):
    sems = refs[-1]
    copies = [
        pltpu.make_async_copy(refs[i], refs[3 + i], sems.at[i]) for i in range(3)
    ]
    for copy in copies:
        copy.start()
    for copy in copies:
        copy.wait()


def on_chip_grid(
    frame_tokens,
    visible,
    grad_output,
    norm_gain,
    query_weight,
    key_weight,
    value_weight,
    output_weight,
):
    tokens = frame_tokens[0]
    frames, cells, width = tokens.shape
    groups = cells // SHARDS
    depth, att = query_weight.shape
    share = output_weight.shape[0]
    local = lax.dynamic_slice_in_dim(visible[0], lax.axis_index("tm") * groups, groups, 1)
    codes = local + 4 * jnp.arange(groups, dtype=jnp.int32)[None]
    codes = jnp.pad(
        codes.reshape(SHARDS, frames * groups),
        ((0, 0), (0, ROWS - frames * groups)),
        constant_values=-1,
    )
    rows = SHARDS * ROWS
    low, high = jnp.bfloat16, jnp.float32
    vmem = pl.BlockSpec(memory_space=pltpu.VMEM)
    dma = pltpu.SemaphoreType.DMA
    wide = pltpu.VMEM((SHARDS, ROWS, width * 4 // 5), low)
    thin = pltpu.VMEM((SHARDS, ROWS, att * 4 // 5), low)
    two_thin = pltpu.VMEM((2, SHARDS, ROWS, att * 4 // 5), low)
    plain = pltpu.VMEM((rows, att), low)
    total = pltpu.VMEM((rows, att), high)
    quarter = pltpu.VMEM((4, 4, share, att), low)
    block_rows, grad_rows, grad_weight = pl.pallas_call(
        fused_kernel,
        out_shape=(
            jax.ShapeDtypeStruct(tokens.shape, low),
            jax.ShapeDtypeStruct(tokens.shape, low),
            jax.ShapeDtypeStruct((share, width), high),
        ),
        in_specs=[vmem] * 8,
        out_specs=(vmem,) * 3,
        scratch_shapes=[
            pltpu.VMEM((4, SHARDS, depth, att), low),
            pltpu.VMEM((1 + frames, rows, frames * cells), low),
            pltpu.VMEM((frames, rows, rows), low),
            wide, wide,
            plain, plain, plain, plain,
            pltpu.VMEM((HEADS, rows, rows), high),
            total, total, total,
            thin, thin, thin, thin, two_thin, two_thin,
            pltpu.VMEM((2, 4, 4, share, att), low),
            quarter, quarter, quarter,
            pltpu.VMEM((4, share, att), low),
            pltpu.VMEM((4, share, att), low),
            pltpu.VMEM((2, share, att), high),
            dma((40,)),
            *[dma((2 * SHARDS,))] * 3,
            *[dma((1,))] * 6,
            *[dma((2,))] * 2,
            *[dma((4,))] * 4,
            dma((2,)),
            dma((2,)),
        ],
        compiler_params=pltpu.CompilerParams(
            collective_id=0, has_side_effects=True, vmem_limit_bytes=56 * 1024 * 1024
        ),
        name="temporal_block",
    )(
        tokens,
        grad_output[0],
        norm_gain,
        codes.reshape(1, rows),
        query_weight,
        key_weight,
        value_weight,
        output_weight,
    )
    anywhere = pl.BlockSpec(memory_space=pl.ANY)
    results = (block_rows, grad_rows, grad_weight)
    block_rows, grad_rows, grad_weight = pl.pallas_call(
        copy_kernel,
        out_shape=tuple(jax.ShapeDtypeStruct(r.shape, r.dtype) for r in results),
        in_specs=[anywhere] * 3,
        out_specs=(anywhere,) * 3,
        scratch_shapes=[dma((3,))],
        name="copy_results",
    )(*results)
    return (block_rows[None], grad_rows[None], grad_weight)


def solution(mesh):
    chip_grid = mesh.shape["tm"] == SHARDS and mesh.shape["dp"] == 2
    return jax.shard_map(
        on_chip_grid if chip_grid else on_device,
        mesh=mesh,
        in_specs=(
            P("dp", "tm", None, None),
            P("dp", None, None),
            P("dp", "tm", None, None),
            P(),
            P("tm", None),
            P("tm", None),
            P("tm", None),
            P("tm", None),
        ),
        out_specs=(P("dp", "tm", None, None), P("dp", "tm", None, None), P("tm", None)),
        check_vma=False,
    )
```

```python
import math

import jax
import jax.numpy as jnp
from jax import lax
from jax.experimental import pallas as pl
from jax.experimental.pallas import tpu as pltpu
from jax.sharding import PartitionSpec as P

HEADS = 8


NORM_EPS = 1e-06


def normalize(token_rows, norm_gain):
    values = token_rows.astype(jnp.float32)
    centered = values - jnp.mean(values, axis=-1, keepdims=True)
    inverse = lax.rsqrt(jnp.mean(centered * centered, axis=-1, keepdims=True) + NORM_EPS)
    scaled = centered * inverse
    return (scaled, inverse, (scaled * norm_gain).astype(jnp.bfloat16))


def project(token_rows, weight):
    lead_shape = token_rows.shape[:-1]
    flat_rows = token_rows.reshape(-1, token_rows.shape[-1])
    result = jnp.dot(flat_rows, weight, preferred_element_type=jnp.float32)
    return result.astype(jnp.bfloat16).reshape(lead_shape + (weight.shape[1],))


def split_heads(values):
    return values.reshape(values.shape[:-1] + (HEADS, values.shape[-1] // HEADS))


def attend(query_rows, key_rows, value_rows, same_cell):
    score_scale = 1.0 / math.sqrt(query_rows.shape[-1] // HEADS)
    query_heads = split_heads(query_rows)
    key_heads = split_heads(key_rows)
    value_heads = split_heads(value_rows)
    scores = (
        jnp.einsum("fghe,tghe->ghft", query_heads, key_heads, preferred_element_type=jnp.float32)
        * score_scale
    )
    scores = jnp.where(same_cell[:, None], scores, -jnp.inf)
    row_top = jnp.max(scores, axis=-1, keepdims=True)
    expons = jnp.exp(scores - row_top)
    soft_probs = expons / jnp.sum(expons, axis=-1, keepdims=True)
    probs_low = soft_probs.astype(jnp.bfloat16)
    mixed_rows = jnp.einsum(
        "ghft,tghe->fghe", probs_low, value_heads, preferred_element_type=jnp.float32
    )
    return (soft_probs, probs_low, mixed_rows.reshape(query_rows.shape).astype(jnp.bfloat16))


def attend_back(query_rows, key_rows, value_rows, soft_probs, probs_low, grad_mixed):
    score_scale = 1.0 / math.sqrt(query_rows.shape[-1] // HEADS)
    query_heads = split_heads(query_rows)
    key_heads = split_heads(key_rows)
    value_heads = split_heads(value_rows)
    grad_heads = split_heads(grad_mixed)
    grad_probs = jnp.einsum(
        "fghe,tghe->ghft", grad_heads, value_heads, preferred_element_type=jnp.float32
    )
    centre = jnp.sum(soft_probs * grad_probs, axis=-1, keepdims=True)
    grad_scores = (soft_probs * (grad_probs - centre) * score_scale).astype(jnp.bfloat16)
    grad_query = jnp.einsum(
        "ghft,tghe->fghe", grad_scores, key_heads, preferred_element_type=jnp.float32
    )
    grad_key = jnp.einsum(
        "ghft,fghe->tghe", grad_scores, query_heads, preferred_element_type=jnp.float32
    )
    grad_value = jnp.einsum(
        "ghft,fghe->tghe", probs_low, grad_heads, preferred_element_type=jnp.float32
    )
    full_shape = query_rows.shape
    return (
        grad_query.reshape(full_shape).astype(jnp.bfloat16),
        grad_key.reshape(full_shape).astype(jnp.bfloat16),
        grad_value.reshape(full_shape).astype(jnp.bfloat16),
    )


def back_project(grad_query, grad_key, grad_value, query_weight, key_weight, value_weight):
    lead_shape = grad_query.shape[:-1]
    width = grad_query.shape[-1]
    total = jnp.dot(
        grad_query.reshape(-1, width), query_weight.T, preferred_element_type=jnp.float32
    )
    total = total + jnp.dot(
        grad_key.reshape(-1, width), key_weight.T, preferred_element_type=jnp.float32
    )
    total = total + jnp.dot(
        grad_value.reshape(-1, width), value_weight.T, preferred_element_type=jnp.float32
    )
    return total.astype(jnp.bfloat16).reshape(lead_shape + (query_weight.shape[0],))


def on_device(
    frame_tokens,
    visible,
    grad_output,
    norm_gain,
    query_weight,
    key_weight,
    value_weight,
    output_weight,
):
    query_weight, key_weight, value_weight, output_weight = (
        lax.all_gather(query_weight, "tm", axis=0, tiled=True),
        lax.all_gather(key_weight, "tm", axis=0, tiled=True),
        lax.all_gather(value_weight, "tm", axis=0, tiled=True),
        lax.all_gather(output_weight, "tm", axis=0, tiled=True),
    )
    shards = lax.axis_size("tm")
    tokens = frame_tokens[0]
    frame_count, visible_count, width = tokens.shape
    att_width = output_weight.shape[0]
    groups = visible_count // shards
    scaled, inverse, normed = normalize(tokens, norm_gain)
    local_cells = lax.dynamic_slice_in_dim(visible[0], lax.axis_index("tm") * groups, groups, 1)
    cell_major = local_cells.T
    same_cell = cell_major[:, :, None] == cell_major[:, None, :]
    query_rows = project(normed, query_weight)
    key_rows = project(normed, key_weight)
    value_rows = project(normed, value_weight)
    query_rows, key_rows, value_rows = (
        lax.all_to_all(query_rows, "tm", split_axis=1, concat_axis=0, tiled=True),
        lax.all_to_all(key_rows, "tm", split_axis=1, concat_axis=0, tiled=True),
        lax.all_to_all(value_rows, "tm", split_axis=1, concat_axis=0, tiled=True),
    )
    soft_probs, probs_low, mixed_cells = attend(query_rows, key_rows, value_rows, same_cell)
    mixed_frames = lax.all_to_all(mixed_cells, "tm", split_axis=0, concat_axis=1, tiled=True)
    flat_mixed = mixed_frames.reshape(-1, att_width)
    flat_tokens = tokens.reshape(-1, width)
    update = jnp.dot(flat_mixed, output_weight, preferred_element_type=jnp.float32)
    block_rows = (
        (flat_tokens.astype(jnp.float32) + update).astype(jnp.bfloat16).reshape(tokens.shape)
    )
    flat_grad = grad_output[0].reshape(-1, width)
    grad_mixed = jnp.dot(flat_grad, output_weight.T, preferred_element_type=jnp.float32)
    grad_mixed = grad_mixed.astype(jnp.bfloat16).reshape(frame_count, visible_count, att_width)
    term_share = lax.psum_scatter(
        jnp.dot(flat_mixed.T, flat_grad, preferred_element_type=jnp.float32),
        "tm",
        scatter_dimension=0,
        tiled=True,
    )
    grad_weight = lax.psum(term_share.astype(jnp.bfloat16), "dp").astype(jnp.float32)
    grad_cells = lax.all_to_all(grad_mixed, "tm", split_axis=1, concat_axis=0, tiled=True)
    grad_query, grad_key, grad_value = attend_back(
        query_rows, key_rows, value_rows, soft_probs, probs_low, grad_cells
    )
    grad_query, grad_key, grad_value = (
        lax.all_to_all(grad_query, "tm", split_axis=0, concat_axis=1, tiled=True),
        lax.all_to_all(grad_key, "tm", split_axis=0, concat_axis=1, tiled=True),
        lax.all_to_all(grad_value, "tm", split_axis=0, concat_axis=1, tiled=True),
    )
    grad_normed = back_project(
        grad_query, grad_key, grad_value, query_weight, key_weight, value_weight
    )
    weighted = grad_normed.astype(jnp.float32) * norm_gain
    first_mean = jnp.mean(weighted, axis=-1, keepdims=True)
    second_mean = jnp.mean(weighted * scaled, axis=-1, keepdims=True)
    grad_rows = inverse * (weighted - first_mean - scaled * second_mean) + grad_output[0].astype(
        jnp.float32
    )
    return (block_rows[None], grad_rows.astype(jnp.bfloat16)[None], grad_weight)


SHARDS = 16
ROWS = 16


def nt_dot(left, right):
    return lax.dot_general(left, right, (((1,), (1,)), ((), ())), preferred_element_type=jnp.float32)


def tn_dot(left, right):
    return lax.dot_general(left, right, (((0,), (0,)), ((), ())), preferred_element_type=jnp.float32)


def nn_dot(left, right):
    return jnp.dot(left, right, preferred_element_type=jnp.float32)


def head_window(head, head_dim):
    low = head * head_dim
    start = low // 128 * 128
    stop = -(-(low + head_dim) // 128) * 128
    lane = lax.broadcasted_iota(jnp.int32, (1, stop - start), 1) + start
    inside = jnp.where((lane >= low) & (lane < low + head_dim), 1.0, 0.0)
    return (slice(start, stop), inside.astype(jnp.bfloat16))


def block_maps(cells, frames, frame_map, cell_map):
    groups = cells // SHARDS
    taken = frames * groups
    place = lax.broadcasted_iota(jnp.int32, (SHARDS * ROWS, 1), 0)
    source = lax.broadcasted_iota(jnp.int32, (1, frames * cells), 1)
    owner, inner = lax.div(place, ROWS), lax.rem(place, ROWS)
    frame, group = lax.div(inner, groups), lax.rem(inner, groups)
    main = inner < taken

    def hits(wanted, valid):
        return jnp.where(jnp.where(valid, wanted, -1) == source, 1.0, 0.0).astype(jnp.bfloat16)

    frame_map[0] = hits(frame * cells + owner * groups + group, main)
    cell_map[0] = hits(owner * taken + inner, main)
    for f in range(frames):
        spare = jnp.logical_not(main)
        frame_map[1 + f] = hits(f * cells + owner * groups + inner - taken, spare)
        cell_map[1 + f] = hits(owner * taken + f * groups + inner - taken, spare)


def fused_kernel(
    tok, gout, gain, code_row, wq, wk, wv, wo,
    block_o, gtok_o, dw_o,
    wall, frame_map, cell_map, norm_s, norm_r, q_s, k_s, v_s, gm_s, probs_s,
    acc_a, acc_b, acc_c, gm_out, gm_in, mix_s, mix_r, gn_s, gn_r,
    dwp, dw_in, dwa_s, dwa_r, dwb_s, dwb_r, dwf,
    w_send, w_recv, sib_send, sib_recv, gm_send, gm_recv, no_send, no_recv,
    mi_send, mi_recv, gn_send, gn_recv, da_send, da_recv, db_send, db_recv, pair_send, pair_recv,
):
    t = lax.axis_index("tm")
    c = lax.axis_index("dp")
    x = lax.rem(t, 2)
    y = lax.rem(lax.div(t, 2), 2)
    z = lax.div(t, 4)
    plane = lax.rem(t, 4)
    xn = t + 1 - 2 * x
    yn = t + 2 - 4 * y
    att = q_s.shape[1]
    frames, cells, width = tok.shape
    count = frames * cells
    depth = wq.shape[0]
    share = wo.shape[0]
    rows = SHARDS * ROWS
    head_dim = att // HEADS
    scale = 1.0 / math.sqrt(head_dim)
    low, high = jnp.bfloat16, jnp.float32

    def to_tm(src, dst, send, recv, peer):
        return pltpu.make_async_remote_copy(
            src_ref=src, dst_ref=dst, send_sem=send, recv_sem=recv,
            device_id={"tm": peer}, device_id_type=pl.DeviceIdType.MESH,
        )

    def to_pair(src, dst, send, recv):
        return pltpu.make_async_remote_copy(
            src_ref=src, dst_ref=dst, send_sem=send, recv_sem=recv,
            device_id={"dp": 1 - c}, device_id_type=pl.DeviceIdType.MESH,
        )

    barrier = pltpu.get_barrier_semaphore()

    @pl.loop(1, SHARDS)
    def _(d):
        pl.semaphore_signal(
            barrier, inc=1, device_id={"tm": lax.rem(t + d, SHARDS)},
            device_id_type=pl.DeviceIdType.MESH,
        )

    pl.semaphore_signal(
        barrier, inc=1, device_id={"dp": 1 - c}, device_id_type=pl.DeviceIdType.MESH
    )
    wall[0, t] = wq[...]
    wall[1, t] = wk[...]
    wall[2, t] = wv[...]
    output_rows = wo[...].astype(high)
    wall[3, t] = jnp.concatenate([output_rows[:, :att], output_rows[:, att:]], axis=0).astype(low)
    pl.semaphore_wait(barrier, SHARDS)

    def item(h, s):
        return wall.at[3 * c if h == 0 else 1 + c, s]

    def pass_item(h, s, peer, kind):
        slot = (h * 5 + kind) * 4 + lax.div(s, 4)
        return to_tm(item(h, s), item(h, s), w_send.at[slot], w_recv.at[h * SHARDS + s], peer)

    def wait_item(h, s):
        pass_item(h, s, xn, 0).wait_recv()

    def pair_item(h, s):
        slot = h * SHARDS + s
        return to_pair(item(h, s), item(h, s), sib_send.at[slot], sib_recv.at[slot])

    def go_up(h, s):
        @pl.when(z < 3)
        def _():
            pass_item(h, s, t + 4, 0).start()

    def go_down(h, s):
        @pl.when(z > 0)
        def _():
            pass_item(h, s, t - 4, 1).start()

    def go_across(h, s):
        pass_item(h, s, xn, 2).start()
        pass_item(h, s, yn, 3).start()

    def at_levels(k, action):
        if k == 0:
            action(t, None)
        else:
            @pl.when(z >= k)
            def _():
                action(t - 4 * k, go_up)

            @pl.when(z + k <= 3)
            def _():
                action(t + 4 * k, go_down)

    def from_column(h, k):
        def action(s, onward):
            wait_item(h, s)
            onward(h, s)
            go_across(h, s)

        at_levels(k, action)

    def from_plane(h, k):
        def action(s, _):
            level = s - plane
            from_x = level + lax.rem(xn, 4)
            from_y = level + lax.rem(yn, 4)
            wait_item(h, from_x)

            @pl.when(c == 0)
            def _():
                pass_item(h, from_x, yn, 4).start()

            wait_item(h, from_y)

            @pl.when(c == 1)
            def _():
                pass_item(h, from_y, xn, 4).start()


        at_levels(k, action)

    def pair_level(h, level):
        return to_pair(
            level_items(c, h, level), level_items(c, h, level),
            sib_send.at[h * SHARDS + level], sib_recv.at[h * SHARDS + level],
        )

    def level_items(core, h, level):
        return wall.at[3 * core if h == 0 else 1 + core, pl.ds(level, 4)]

    def from_across(h, k):
        def action(s, _):
            level = s - plane
            wait_item(h, level + 3 - plane)
            if k == 0:
                for d in range(1, 4):
                    pair_item(h, level + lax.rem(plane + d, 4)).start()
            else:
                pair_level(h, level).start()

        at_levels(k, action)

    def send_own(h):
        go_up(h, t)
        go_down(h, t)
        go_across(h, t)

    def wait_pair(h):
        def action(s, _):
            level = s - plane
            if s is t:
                for d in range(1, 4):
                    mate = level + lax.rem(plane + d, 4)
                    slot = h * SHARDS + mate
                    landed = wall.at[3 * (1 - c) if h == 0 else 2 - c, mate]
                    to_pair(landed, landed, sib_send.at[slot], sib_recv.at[slot]).wait_recv()
            else:
                slot = h * SHARDS + level
                landed = level_items(1 - c, h, level)
                to_pair(landed, landed, sib_send.at[slot], sib_recv.at[slot]).wait_recv()

        for k in range(4):
            at_levels(k, action)

    send_own(0)

    def send_peers(src, dst, send, recv):
        @pl.loop(1, SHARDS)
        def _(d):
            peer = lax.rem(t + d, SHARDS)
            to_tm(src.at[peer], dst.at[t], send.at[0], recv.at[0], peer).start()

        dst[t] = src[t]

    def wait_peers(src, dst, send, recv, sends):
        others = pl.ds(0, SHARDS - 1)
        copies = to_tm(src.at[others], dst.at[others], send.at[0], recv.at[0], xn)
        if sends:
            copies.wait_send()
        else:
            copies.wait_recv()

    block_maps(cells, frames, frame_map, cell_map)

    def pack(row_map, values, out):
        columns = values.shape[1]
        tail = columns // 5
        packed = nn_dot(row_map[0], values[:, : columns - tail])
        spare = [nn_dot(row_map[1 + f], values[:, columns - tail :]) for f in range(frames)]
        spare.append(jnp.zeros((rows, columns - tail - frames * tail), high))
        packed = packed + jnp.concatenate(spare, axis=1)
        out[...] = packed.astype(low).reshape(out.shape)

    def unpack(row_map, packed):
        columns = packed.shape[2] * 5 // 4
        tail = columns // 5
        values = packed[...].reshape(rows, columns - tail)
        main = tn_dot(row_map[0], values)
        last = sum(tn_dot(row_map[1 + f], values[:, f * tail : (f + 1) * tail]) for f in range(frames))
        return jnp.concatenate([main, last], axis=1)

    def norm_rows():
        values = tok[...].reshape(count, width).astype(high)
        centered = values - jnp.mean(values, axis=-1, keepdims=True)
        inverse = lax.rsqrt(jnp.mean(centered * centered, axis=-1, keepdims=True) + NORM_EPS)
        return (centered * inverse, inverse)

    gains = gain[...].reshape(1, width)
    pack(frame_map, (norm_rows()[0] * gains).astype(low), norm_s)
    send_peers(norm_s, norm_r, no_send, no_recv)

    from_column(0, 1)
    send_own(1)
    from_plane(0, 0)
    from_column(0, 2)
    from_column(1, 1)
    from_plane(0, 1)
    from_plane(1, 0)
    from_across(0, 0)
    from_column(0, 3)
    from_column(1, 2)
    from_plane(0, 2)
    from_plane(1, 1)
    from_across(0, 1)
    from_across(1, 0)
    from_column(1, 3)
    from_plane(0, 3)
    from_plane(1, 2)
    from_across(0, 2)
    from_across(1, 1)
    from_plane(1, 3)
    from_across(0, 3)
    wait_pair(0)

    def full(j):
        return wall[j].reshape(SHARDS * depth, att)

    def output_half(j):
        blocks = wall[3].astype(high)[:, j * share : (j + 1) * share]
        return blocks.reshape(SHARDS * share, att).astype(low)

    grads = gout[...].reshape(count, width)
    grad_mixed = nt_dot(grads[:, :att], output_half(0)) + nt_dot(grads[:, att:], output_half(1))
    pack(frame_map, grad_mixed.astype(low), gm_out)
    send_peers(gm_out, gm_in, gm_send, gm_recv)

    from_across(1, 2)
    from_across(1, 3)
    wait_peers(norm_s, norm_r, no_send, no_recv, False)
    normed = unpack(cell_map, norm_r).astype(low)
    q_s[...] = nn_dot(normed, full(0)).astype(low)
    wait_pair(1)
    k_s[...] = nn_dot(normed, full(1)).astype(low)
    v_s[...] = nn_dot(normed, full(2)).astype(low)

    codes = jnp.broadcast_to(code_row[...].astype(high), (rows, rows))
    same = (codes == codes.T)[:count, :count]
    acc_a[...] = jnp.zeros_like(acc_a)
    for head in range(HEADS):
        window, inside = head_window(head, head_dim)
        scores = nt_dot(q_s[:, window] * inside, k_s[:, window]) * scale
        scores = jnp.where(same, scores, -jnp.inf)
        expons = jnp.exp(scores - jnp.max(scores, axis=-1, keepdims=True))
        probs = expons * (1.0 / jnp.sum(expons, axis=-1, keepdims=True))
        probs_s[head] = probs
        acc_a[:, window] += nn_dot(probs.astype(low), v_s[:, window] * inside)
    pack(cell_map, acc_a[...].astype(low), mix_s)
    send_peers(mix_s, mix_r, mi_send, mi_recv)

    wait_peers(gm_out, gm_in, gm_send, gm_recv, False)
    gm_s[...] = unpack(cell_map, gm_in).astype(low)

    acc_a[...] = jnp.zeros_like(acc_a)
    acc_b[...] = jnp.zeros_like(acc_b)
    acc_c[...] = jnp.zeros_like(acc_c)
    def back_head(head):
        window, inside = head_window(head, head_dim)
        grad_head = gm_s[:, window] * inside
        probs = probs_s[head]
        grad_probs = nt_dot(grad_head, v_s[:, window])
        centre = jnp.sum(probs * grad_probs, axis=-1, keepdims=True)
        grad_scores = (probs * (grad_probs - centre) * scale).astype(low)
        acc_a[:, window] += nn_dot(grad_scores, k_s[:, window] * inside)
        acc_b[:, window] += tn_dot(grad_scores, q_s[:, window] * inside)
        acc_c[:, window] += tn_dot(probs.astype(low), grad_head)

    for head in range(HEADS // 2):
        back_head(head)

    wait_peers(mix_s, mix_r, mi_send, mi_recv, False)
    mixed_frames = unpack(frame_map, mix_r).astype(low)
    for j in range(2):
        term = tn_dot(mixed_frames, grads[:, j * att : (j + 1) * att])
        term = term.reshape(4, 4, share, att).astype(low)
        for level in range(4):
            for place in range(4):
                dwp[j, place, level] = term[level, place]
    pair_term = to_pair(dwp.at[1 - c], dw_in, pair_send.at[0], pair_recv.at[0])
    pair_term.start()

    for head in range(HEADS // 2, HEADS):
        back_head(head)

    def mate_copy(d):
        mate = lax.rem(plane + d, 4)
        return to_tm(dwa_s.at[mate], dwa_r.at[plane], da_send.at[mate], da_recv.at[plane], z * 4 + mate)

    pair_term.wait_recv()

    @pl.loop(0, 4)
    def _(place):
        both = dwp[c, place].astype(high) + dw_in[place].astype(high)
        dwa_s[place] = both.astype(low)

    for d in range(1, 4):
        mate_copy(d).start()
    dwa_r[plane] = dwa_s[plane]

    grad_rows = [acc[...].astype(low) for acc in (acc_a, acc_b, acc_c)]
    for j in range(2):
        shards = slice(j * SHARDS // 2, (j + 1) * SHARDS // 2)
        total = sum(
            nt_dot(grad_rows[i], wall[i, shards].reshape(SHARDS // 2 * depth, att)) for i in range(3)
        )
        pack(cell_map, total.astype(low), gn_s.at[j])
        send_peers(gn_s.at[j], gn_r.at[j], gn_send.at[pl.ds(j, 1)], gn_recv.at[pl.ds(j, 1)])

    for j in range(2):
        columns = slice(j * att, (j + 1) * att)
        update = nn_dot(mixed_frames, output_half(j))
        rows_out = tok[:, :, columns].reshape(count, att).astype(high) + update
        block_o[:, :, columns] = rows_out.astype(low).reshape(frames, cells, att)
    scaled, inverse = norm_rows()

    def finish_items(h):
        pass_item(h, t, xn, 2).wait_send()
        pass_item(h, t, yn, 3).wait_send()
        for level in range(4):
            @pl.when((z < 3) & (level <= z))
            def _():
                pass_item(h, level * 4 + plane, xn, 0).wait_send()

            @pl.when((z > 0) & (level >= z))
            def _():
                pass_item(h, level * 4 + plane, xn, 1).wait_send()

            @pl.when(level != z)
            def _():
                pass_item(h, level * 4 + plane, xn, 2).wait_send()
                pass_item(h, level * 4 + plane, yn, 3).wait_send()
                pair_level(h, level * 4).wait_send()

            pass_item(h, level * 4 + plane, xn, 4).wait_send()
        for d in range(1, 4):
            pair_item(h, z * 4 + lax.rem(plane + d, 4)).wait_send()

    def level_copy(d):
        level = lax.rem(z + d, 4)
        return to_tm(dwb_s.at[level], dwb_r.at[z], db_send.at[level], db_recv.at[z], level * 4 + plane)

    for d in range(1, 4):
        mate = lax.rem(plane + d, 4)
        to_tm(dwa_s.at[mate], dwa_r.at[mate], da_send.at[mate], da_recv.at[mate], z * 4 + mate).wait_recv()
    dwb_s[...] = jnp.sum(dwa_r[...].astype(high), axis=0).astype(low)
    for d in range(1, 4):
        level_copy(d).start()
    dwb_r[z] = dwb_s[z]

    pair_term.wait_send()
    for h in range(2):
        finish_items(h)
    for d in range(1, 4):
        mate_copy(d).wait_send()
    wait_peers(gm_out, gm_in, gm_send, gm_recv, True)
    wait_peers(norm_s, norm_r, no_send, no_recv, True)
    wait_peers(mix_s, mix_r, mi_send, mi_recv, True)

    grad_parts = []
    for j in range(2):
        sems = (gn_send.at[pl.ds(j, 1)], gn_recv.at[pl.ds(j, 1)])
        wait_peers(gn_s.at[j], gn_r.at[j], *sems, False)
        grad_parts.append(unpack(frame_map, gn_r.at[j]))
    weighted = jnp.concatenate(grad_parts, axis=1) * gains
    first = jnp.mean(weighted, axis=-1, keepdims=True)
    second = jnp.mean(weighted * scaled, axis=-1, keepdims=True)
    result = inverse * (weighted - first - scaled * second)
    result = result + gout[...].reshape(count, width).astype(high)
    gtok_o[...] = result.astype(low).reshape(frames, cells, width)

    for d in range(1, 4):
        level = lax.rem(z + d, 4)
        to_tm(dwb_s.at[level], dwb_r.at[level], db_send.at[level], db_recv.at[level], level * 4 + plane).wait_recv()
    dwf[c] = jnp.sum(dwb_r[...].astype(high), axis=0)
    pair_sum = to_pair(dwf.at[c], dwf.at[c], pair_send.at[1], pair_recv.at[1])
    pair_sum.start()

    to_pair(dwf.at[1 - c], dwf.at[1 - c], pair_send.at[1], pair_recv.at[1]).wait_recv()
    dw_o[:, :att] = dwf[0]
    dw_o[:, att:] = dwf[1]

    pair_sum.wait_send()
    for d in range(1, 4):
        level_copy(d).wait_send()
    for j in range(2):
        sems = (gn_send.at[pl.ds(j, 1)], gn_recv.at[pl.ds(j, 1)])
        wait_peers(gn_s.at[j], gn_r.at[j], *sems, True)


def copy_kernel(*refs):
    for source, target in zip(refs[:3], refs[3:]):
        target[...] = source[...]


def on_chip_grid(
    frame_tokens,
    visible,
    grad_output,
    norm_gain,
    query_weight,
    key_weight,
    value_weight,
    output_weight,
):
    tokens = frame_tokens[0]
    frames, cells, width = tokens.shape
    groups = cells // SHARDS
    depth, att = query_weight.shape
    share = output_weight.shape[0]
    local = lax.dynamic_slice_in_dim(visible[0], lax.axis_index("tm") * groups, groups, 1)
    codes = local + 4 * jnp.arange(groups, dtype=jnp.int32)[None]
    rows, count = SHARDS * ROWS, frames * cells
    codes = jnp.pad(codes.reshape(1, count), ((0, 0), (0, rows - count)), constant_values=-1)
    low, high = jnp.bfloat16, jnp.float32
    vmem = pl.BlockSpec(memory_space=pltpu.VMEM)
    dma = pltpu.SemaphoreType.DMA
    wide = pltpu.VMEM((SHARDS, ROWS, width * 4 // 5), low)
    thin = pltpu.VMEM((SHARDS, ROWS, att * 4 // 5), low)
    two_thin = pltpu.VMEM((2, SHARDS, ROWS, att * 4 // 5), low)
    plain = pltpu.VMEM((count, att), low)
    total = pltpu.VMEM((count, att), high)
    quarter = pltpu.VMEM((4, 4, share, att), low)
    block_rows, grad_rows, grad_weight = pl.pallas_call(
        fused_kernel,
        out_shape=(
            jax.ShapeDtypeStruct(tokens.shape, low),
            jax.ShapeDtypeStruct(tokens.shape, low),
            jax.ShapeDtypeStruct((share, width), high),
        ),
        in_specs=[vmem] * 8,
        out_specs=(vmem,) * 3,
        scratch_shapes=[
            pltpu.VMEM((4, SHARDS, depth, att), low),
            pltpu.VMEM((1 + frames, rows, count), low),
            pltpu.VMEM((1 + frames, rows, count), low),
            wide, wide,
            plain, plain, plain, plain,
            pltpu.VMEM((HEADS, count, count), high),
            total, total, total,
            thin, thin, thin, thin, two_thin, two_thin,
            pltpu.VMEM((2, 4, 4, share, att), low),
            quarter, quarter, quarter,
            pltpu.VMEM((4, share, att), low),
            pltpu.VMEM((4, share, att), low),
            pltpu.VMEM((2, share, att), high),
            dma((40,)),
            *[dma((2 * SHARDS,))] * 3,
            *[dma((1,))] * 6,
            *[dma((2,))] * 2,
            *[dma((4,))] * 4,
            dma((2,)),
            dma((2,)),
        ],
        compiler_params=pltpu.CompilerParams(
            collective_id=0, has_side_effects=True, vmem_limit_bytes=40 * 1024 * 1024
        ),
        name="temporal_block",
    )(
        tokens,
        grad_output[0],
        norm_gain,
        codes,
        query_weight,
        key_weight,
        value_weight,
        output_weight,
    )
    results = (block_rows, grad_rows, grad_weight)
    block_rows, grad_rows, grad_weight = pl.pallas_call(
        copy_kernel,
        out_shape=tuple(jax.ShapeDtypeStruct(r.shape, r.dtype) for r in results),
        in_specs=[vmem] * 3,
        out_specs=(vmem,) * 3,
        name="copy_results",
    )(*results)
    return (block_rows[None], grad_rows[None], grad_weight)


def solution(mesh):
    chip_grid = mesh.shape["tm"] == SHARDS and mesh.shape["dp"] == 2
    return jax.shard_map(
        on_chip_grid if chip_grid else on_device,
        mesh=mesh,
        in_specs=(
            P("dp", "tm", None, None),
            P("dp", None, None),
            P("dp", "tm", None, None),
            P(),
            P("tm", None),
            P("tm", None),
            P("tm", None),
            P("tm", None),
        ),
        out_specs=(P("dp", "tm", None, None), P("dp", "tm", None, None), P("tm", None)),
        check_vma=False,
    )
```

```python
import math

import jax
import jax.numpy as jnp
from jax import lax
from jax.experimental import pallas as pl
from jax.experimental.pallas import tpu as pltpu
from jax.sharding import PartitionSpec as P

HEADS = 8


NORM_EPS = 1e-06


def normalize(token_rows, norm_gain):
    values = token_rows.astype(jnp.float32)
    centered = values - jnp.mean(values, axis=-1, keepdims=True)
    inverse = lax.rsqrt(jnp.mean(centered * centered, axis=-1, keepdims=True) + NORM_EPS)
    scaled = centered * inverse
    return (scaled, inverse, (scaled * norm_gain).astype(jnp.bfloat16))


def project(token_rows, weight):
    lead_shape = token_rows.shape[:-1]
    flat_rows = token_rows.reshape(-1, token_rows.shape[-1])
    result = jnp.dot(flat_rows, weight, preferred_element_type=jnp.float32)
    return result.astype(jnp.bfloat16).reshape(lead_shape + (weight.shape[1],))


def split_heads(values):
    return values.reshape(values.shape[:-1] + (HEADS, values.shape[-1] // HEADS))


def attend(query_rows, key_rows, value_rows, same_cell):
    score_scale = 1.0 / math.sqrt(query_rows.shape[-1] // HEADS)
    query_heads = split_heads(query_rows)
    key_heads = split_heads(key_rows)
    value_heads = split_heads(value_rows)
    scores = (
        jnp.einsum("fghe,tghe->ghft", query_heads, key_heads, preferred_element_type=jnp.float32)
        * score_scale
    )
    scores = jnp.where(same_cell[:, None], scores, -jnp.inf)
    row_top = jnp.max(scores, axis=-1, keepdims=True)
    expons = jnp.exp(scores - row_top)
    soft_probs = expons / jnp.sum(expons, axis=-1, keepdims=True)
    probs_low = soft_probs.astype(jnp.bfloat16)
    mixed_rows = jnp.einsum(
        "ghft,tghe->fghe", probs_low, value_heads, preferred_element_type=jnp.float32
    )
    return (soft_probs, probs_low, mixed_rows.reshape(query_rows.shape).astype(jnp.bfloat16))


def attend_back(query_rows, key_rows, value_rows, soft_probs, probs_low, grad_mixed):
    score_scale = 1.0 / math.sqrt(query_rows.shape[-1] // HEADS)
    query_heads = split_heads(query_rows)
    key_heads = split_heads(key_rows)
    value_heads = split_heads(value_rows)
    grad_heads = split_heads(grad_mixed)
    grad_probs = jnp.einsum(
        "fghe,tghe->ghft", grad_heads, value_heads, preferred_element_type=jnp.float32
    )
    centre = jnp.sum(soft_probs * grad_probs, axis=-1, keepdims=True)
    grad_scores = (soft_probs * (grad_probs - centre) * score_scale).astype(jnp.bfloat16)
    grad_query = jnp.einsum(
        "ghft,tghe->fghe", grad_scores, key_heads, preferred_element_type=jnp.float32
    )
    grad_key = jnp.einsum(
        "ghft,fghe->tghe", grad_scores, query_heads, preferred_element_type=jnp.float32
    )
    grad_value = jnp.einsum(
        "ghft,fghe->tghe", probs_low, grad_heads, preferred_element_type=jnp.float32
    )
    full_shape = query_rows.shape
    return (
        grad_query.reshape(full_shape).astype(jnp.bfloat16),
        grad_key.reshape(full_shape).astype(jnp.bfloat16),
        grad_value.reshape(full_shape).astype(jnp.bfloat16),
    )


def back_project(grad_query, grad_key, grad_value, query_weight, key_weight, value_weight):
    lead_shape = grad_query.shape[:-1]
    width = grad_query.shape[-1]
    total = jnp.dot(
        grad_query.reshape(-1, width), query_weight.T, preferred_element_type=jnp.float32
    )
    total = total + jnp.dot(
        grad_key.reshape(-1, width), key_weight.T, preferred_element_type=jnp.float32
    )
    total = total + jnp.dot(
        grad_value.reshape(-1, width), value_weight.T, preferred_element_type=jnp.float32
    )
    return total.astype(jnp.bfloat16).reshape(lead_shape + (query_weight.shape[0],))


def on_device(
    frame_tokens,
    visible,
    grad_output,
    norm_gain,
    query_weight,
    key_weight,
    value_weight,
    output_weight,
):
    query_weight, key_weight, value_weight, output_weight = (
        lax.all_gather(query_weight, "tm", axis=0, tiled=True),
        lax.all_gather(key_weight, "tm", axis=0, tiled=True),
        lax.all_gather(value_weight, "tm", axis=0, tiled=True),
        lax.all_gather(output_weight, "tm", axis=0, tiled=True),
    )
    shards = lax.axis_size("tm")
    tokens = frame_tokens[0]
    frame_count, visible_count, width = tokens.shape
    att_width = output_weight.shape[0]
    groups = visible_count // shards
    scaled, inverse, normed = normalize(tokens, norm_gain)
    local_cells = lax.dynamic_slice_in_dim(visible[0], lax.axis_index("tm") * groups, groups, 1)
    cell_major = local_cells.T
    same_cell = cell_major[:, :, None] == cell_major[:, None, :]
    query_rows = project(normed, query_weight)
    key_rows = project(normed, key_weight)
    value_rows = project(normed, value_weight)
    query_rows, key_rows, value_rows = (
        lax.all_to_all(query_rows, "tm", split_axis=1, concat_axis=0, tiled=True),
        lax.all_to_all(key_rows, "tm", split_axis=1, concat_axis=0, tiled=True),
        lax.all_to_all(value_rows, "tm", split_axis=1, concat_axis=0, tiled=True),
    )
    soft_probs, probs_low, mixed_cells = attend(query_rows, key_rows, value_rows, same_cell)
    mixed_frames = lax.all_to_all(mixed_cells, "tm", split_axis=0, concat_axis=1, tiled=True)
    flat_mixed = mixed_frames.reshape(-1, att_width)
    flat_tokens = tokens.reshape(-1, width)
    update = jnp.dot(flat_mixed, output_weight, preferred_element_type=jnp.float32)
    block_rows = (
        (flat_tokens.astype(jnp.float32) + update).astype(jnp.bfloat16).reshape(tokens.shape)
    )
    flat_grad = grad_output[0].reshape(-1, width)
    grad_mixed = jnp.dot(flat_grad, output_weight.T, preferred_element_type=jnp.float32)
    grad_mixed = grad_mixed.astype(jnp.bfloat16).reshape(frame_count, visible_count, att_width)
    term_share = lax.psum_scatter(
        jnp.dot(flat_mixed.T, flat_grad, preferred_element_type=jnp.float32),
        "tm",
        scatter_dimension=0,
        tiled=True,
    )
    grad_weight = lax.psum(term_share.astype(jnp.bfloat16), "dp").astype(jnp.float32)
    grad_cells = lax.all_to_all(grad_mixed, "tm", split_axis=1, concat_axis=0, tiled=True)
    grad_query, grad_key, grad_value = attend_back(
        query_rows, key_rows, value_rows, soft_probs, probs_low, grad_cells
    )
    grad_query, grad_key, grad_value = (
        lax.all_to_all(grad_query, "tm", split_axis=0, concat_axis=1, tiled=True),
        lax.all_to_all(grad_key, "tm", split_axis=0, concat_axis=1, tiled=True),
        lax.all_to_all(grad_value, "tm", split_axis=0, concat_axis=1, tiled=True),
    )
    grad_normed = back_project(
        grad_query, grad_key, grad_value, query_weight, key_weight, value_weight
    )
    weighted = grad_normed.astype(jnp.float32) * norm_gain
    first_mean = jnp.mean(weighted, axis=-1, keepdims=True)
    second_mean = jnp.mean(weighted * scaled, axis=-1, keepdims=True)
    grad_rows = inverse * (weighted - first_mean - scaled * second_mean) + grad_output[0].astype(
        jnp.float32
    )
    return (block_rows[None], grad_rows.astype(jnp.bfloat16)[None], grad_weight)


SHARDS = 16
ROWS = 16


def nt_dot(left, right):
    return lax.dot_general(left, right, (((1,), (1,)), ((), ())), preferred_element_type=jnp.float32)


def tn_dot(left, right):
    return lax.dot_general(left, right, (((0,), (0,)), ((), ())), preferred_element_type=jnp.float32)


def nn_dot(left, right):
    return jnp.dot(left, right, preferred_element_type=jnp.float32)


def head_window(head, head_dim):
    low = head * head_dim
    start = low // 128 * 128
    stop = -(-(low + head_dim) // 128) * 128
    lane = lax.broadcasted_iota(jnp.int32, (1, stop - start), 1) + start
    inside = jnp.where((lane >= low) & (lane < low + head_dim), 1.0, 0.0)
    return (slice(start, stop), inside.astype(jnp.bfloat16))


def block_maps(cells, frames, frame_map, cell_map):
    groups = cells // SHARDS
    taken = frames * groups
    place = lax.broadcasted_iota(jnp.int32, (SHARDS * ROWS, 1), 0)
    source = lax.broadcasted_iota(jnp.int32, (1, frames * cells), 1)
    owner, inner = lax.div(place, ROWS), lax.rem(place, ROWS)
    frame, group = lax.div(inner, groups), lax.rem(inner, groups)
    main = inner < taken

    def hits(wanted, valid):
        return jnp.where(jnp.where(valid, wanted, -1) == source, 1.0, 0.0).astype(jnp.bfloat16)

    frame_map[0] = hits(frame * cells + owner * groups + group, main)
    cell_map[0] = hits(owner * taken + inner, main)
    for f in range(frames):
        spare = jnp.logical_not(main)
        frame_map[1 + f] = hits(f * cells + owner * groups + inner - taken, spare)
        cell_map[1 + f] = hits(owner * taken + f * groups + inner - taken, spare)


def fused_kernel(
    tok_h, gout_h, gain, code_row, wq, wk, wv, wo_h,
    block_h, gtok_h, dw_h,
    tok, gout, wo, block_o, gtok_o, dw_o, wall, frame_map, cell_map, norm_s, norm_r, q_s, k_s, v_s, gm_s, probs_s,
    acc_a, acc_b, acc_c, gm_out, gm_in, mix_s, mix_r, gn_s, gn_r,
    dwp, dw_in, dwa_s, dwa_r, dwb_s, dwb_r, dwf,
    w_send, w_recv, sib_send, sib_recv, gm_send, gm_recv, no_send, no_recv,
    mi_send, mi_recv, gn_send, gn_recv, da_send, da_recv, db_send, db_recv, pair_send, pair_recv, load_sem, store_sem,
):
    t = lax.axis_index("tm")
    c = lax.axis_index("dp")
    x = lax.rem(t, 2)
    y = lax.rem(lax.div(t, 2), 2)
    z = lax.div(t, 4)
    plane = lax.rem(t, 4)
    xn = t + 1 - 2 * x
    yn = t + 2 - 4 * y
    att = q_s.shape[1]
    frames, cells, width = tok.shape
    count = frames * cells
    depth = wq.shape[0]
    share = wo.shape[0]
    rows = SHARDS * ROWS
    head_dim = att // HEADS
    scale = 1.0 / math.sqrt(head_dim)
    low, high = jnp.bfloat16, jnp.float32

    def to_tm(src, dst, send, recv, peer):
        return pltpu.make_async_remote_copy(
            src_ref=src, dst_ref=dst, send_sem=send, recv_sem=recv,
            device_id={"tm": peer}, device_id_type=pl.DeviceIdType.MESH,
        )

    def to_pair(src, dst, send, recv):
        return pltpu.make_async_remote_copy(
            src_ref=src, dst_ref=dst, send_sem=send, recv_sem=recv,
            device_id={"dp": 1 - c}, device_id_type=pl.DeviceIdType.MESH,
        )

    own = [wall.at[j, t] for j in range(3)]
    sources = (wq, wk, wv, wo_h, tok_h, gout_h)
    loads = [
        pltpu.make_async_copy(source, target, load_sem.at[i])
        for i, (source, target) in enumerate(zip(sources, (*own, wo, tok, gout)))
    ]
    for load in loads:
        load.start()
    stores = [
        pltpu.make_async_copy(source, target, store_sem.at[i])
        for i, (source, target) in enumerate(((block_o, block_h), (gtok_o, gtok_h), (dw_o, dw_h)))
    ]
    barrier = pltpu.get_barrier_semaphore()

    @pl.loop(1, SHARDS)
    def _(d):
        pl.semaphore_signal(
            barrier, inc=1, device_id={"tm": lax.rem(t + d, SHARDS)},
            device_id_type=pl.DeviceIdType.MESH,
        )

    pl.semaphore_signal(
        barrier, inc=1, device_id={"dp": 1 - c}, device_id_type=pl.DeviceIdType.MESH
    )
    for load in loads[:4]:
        load.wait()
    output_rows = wo[...].astype(high)
    wall[3, t] = jnp.concatenate([output_rows[:, :att], output_rows[:, att:]], axis=0).astype(low)
    pl.semaphore_wait(barrier, SHARDS)

    def item(h, s):
        return wall.at[3 * c if h == 0 else 1 + c, s]

    def pass_item(h, s, peer, kind):
        slot = (h * 5 + kind) * 4 + lax.div(s, 4)
        return to_tm(item(h, s), item(h, s), w_send.at[slot], w_recv.at[h * SHARDS + s], peer)

    def wait_item(h, s):
        pass_item(h, s, xn, 0).wait_recv()

    def pair_item(h, s):
        slot = h * SHARDS + s
        return to_pair(item(h, s), item(h, s), sib_send.at[slot], sib_recv.at[slot])

    def go_up(h, s):
        @pl.when(z < 3)
        def _():
            pass_item(h, s, t + 4, 0).start()

    def go_down(h, s):
        @pl.when(z > 0)
        def _():
            pass_item(h, s, t - 4, 1).start()

    def go_across(h, s):
        pass_item(h, s, xn, 2).start()
        pass_item(h, s, yn, 3).start()

    def at_levels(k, action):
        if k == 0:
            action(t, None)
        else:
            @pl.when(z >= k)
            def _():
                action(t - 4 * k, go_up)

            @pl.when(z + k <= 3)
            def _():
                action(t + 4 * k, go_down)

    def from_column(h, k):
        def action(s, onward):
            wait_item(h, s)
            onward(h, s)
            go_across(h, s)

        at_levels(k, action)

    def from_plane(h, k):
        def action(s, _):
            level = s - plane
            from_x = level + lax.rem(xn, 4)
            from_y = level + lax.rem(yn, 4)
            wait_item(h, from_x)

            @pl.when(c == 0)
            def _():
                pass_item(h, from_x, yn, 4).start()

            wait_item(h, from_y)

            @pl.when(c == 1)
            def _():
                pass_item(h, from_y, xn, 4).start()


        at_levels(k, action)

    def pair_level(h, level):
        return to_pair(
            level_items(c, h, level), level_items(c, h, level),
            sib_send.at[h * SHARDS + level], sib_recv.at[h * SHARDS + level],
        )

    def level_items(core, h, level):
        return wall.at[3 * core if h == 0 else 1 + core, pl.ds(level, 4)]

    def from_across(h, k):
        def action(s, _):
            level = s - plane
            wait_item(h, level + 3 - plane)
            if k == 0:
                for d in range(1, 4):
                    pair_item(h, level + lax.rem(plane + d, 4)).start()
            else:
                pair_level(h, level).start()

        at_levels(k, action)

    def send_own(h):
        go_up(h, t)
        go_down(h, t)
        go_across(h, t)

    def wait_pair(h):
        def action(s, _):
            level = s - plane
            if s is t:
                for d in range(1, 4):
                    mate = level + lax.rem(plane + d, 4)
                    slot = h * SHARDS + mate
                    landed = wall.at[3 * (1 - c) if h == 0 else 2 - c, mate]
                    to_pair(landed, landed, sib_send.at[slot], sib_recv.at[slot]).wait_recv()
            else:
                slot = h * SHARDS + level
                landed = level_items(1 - c, h, level)
                to_pair(landed, landed, sib_send.at[slot], sib_recv.at[slot]).wait_recv()

        for k in range(4):
            at_levels(k, action)

    send_own(0)

    def send_peers(src, dst, send, recv):
        @pl.loop(1, SHARDS)
        def _(d):
            peer = lax.rem(t + d, SHARDS)
            to_tm(src.at[peer], dst.at[t], send.at[0], recv.at[0], peer).start()

        dst[t] = src[t]

    def wait_peers(src, dst, send, recv, sends):
        others = pl.ds(0, SHARDS - 1)
        copies = to_tm(src.at[others], dst.at[others], send.at[0], recv.at[0], xn)
        if sends:
            copies.wait_send()
        else:
            copies.wait_recv()

    block_maps(cells, frames, frame_map, cell_map)

    def pack(row_map, values, out):
        columns = values.shape[1]
        tail = columns // 5
        packed = nn_dot(row_map[0], values[:, : columns - tail])
        spare = [nn_dot(row_map[1 + f], values[:, columns - tail :]) for f in range(frames)]
        spare.append(jnp.zeros((rows, columns - tail - frames * tail), high))
        packed = packed + jnp.concatenate(spare, axis=1)
        out[...] = packed.astype(low).reshape(out.shape)

    def unpack(row_map, packed):
        columns = packed.shape[2] * 5 // 4
        tail = columns // 5
        values = packed[...].reshape(rows, columns - tail)
        main = tn_dot(row_map[0], values)
        last = sum(tn_dot(row_map[1 + f], values[:, f * tail : (f + 1) * tail]) for f in range(frames))
        return jnp.concatenate([main, last], axis=1)

    def norm_rows():
        values = tok[...].reshape(count, width).astype(high)
        centered = values - jnp.mean(values, axis=-1, keepdims=True)
        inverse = lax.rsqrt(jnp.mean(centered * centered, axis=-1, keepdims=True) + NORM_EPS)
        return (centered * inverse, inverse)

    gains = gain[...].reshape(1, width)
    loads[4].wait()
    pack(frame_map, (norm_rows()[0] * gains).astype(low), norm_s)
    send_peers(norm_s, norm_r, no_send, no_recv)

    from_column(0, 1)
    send_own(1)
    from_plane(0, 0)
    from_column(0, 2)
    from_column(1, 1)
    from_plane(0, 1)
    from_plane(1, 0)
    from_across(0, 0)
    from_column(0, 3)
    from_column(1, 2)
    from_plane(0, 2)
    from_plane(1, 1)
    from_across(0, 1)
    from_across(1, 0)
    from_column(1, 3)
    from_plane(0, 3)
    from_plane(1, 2)
    from_across(0, 2)
    from_across(1, 1)
    from_plane(1, 3)
    from_across(0, 3)
    wait_pair(0)

    def full(j):
        return wall[j].reshape(SHARDS * depth, att)

    def output_half(j):
        blocks = wall[3].astype(high)[:, j * share : (j + 1) * share]
        return blocks.reshape(SHARDS * share, att).astype(low)

    loads[5].wait()
    grads = gout[...].reshape(count, width)
    grad_mixed = nt_dot(grads[:, :att], output_half(0)) + nt_dot(grads[:, att:], output_half(1))
    pack(frame_map, grad_mixed.astype(low), gm_out)
    send_peers(gm_out, gm_in, gm_send, gm_recv)

    from_across(1, 2)
    from_across(1, 3)
    wait_peers(norm_s, norm_r, no_send, no_recv, False)
    normed = unpack(cell_map, norm_r).astype(low)
    q_s[...] = nn_dot(normed, full(0)).astype(low)
    wait_pair(1)
    k_s[...] = nn_dot(normed, full(1)).astype(low)
    v_s[...] = nn_dot(normed, full(2)).astype(low)

    codes = jnp.broadcast_to(code_row[...].astype(high), (rows, rows))
    same = (codes == codes.T)[:count, :count]
    acc_a[...] = jnp.zeros_like(acc_a)
    for head in range(HEADS):
        window, inside = head_window(head, head_dim)
        scores = nt_dot(q_s[:, window] * inside, k_s[:, window]) * scale
        scores = jnp.where(same, scores, -jnp.inf)
        expons = jnp.exp(scores - jnp.max(scores, axis=-1, keepdims=True))
        probs = expons * (1.0 / jnp.sum(expons, axis=-1, keepdims=True))
        probs_s[head] = probs
        acc_a[:, window] += nn_dot(probs.astype(low), v_s[:, window] * inside)
    pack(cell_map, acc_a[...].astype(low), mix_s)
    send_peers(mix_s, mix_r, mi_send, mi_recv)

    wait_peers(gm_out, gm_in, gm_send, gm_recv, False)
    gm_s[...] = unpack(cell_map, gm_in).astype(low)

    acc_a[...] = jnp.zeros_like(acc_a)
    acc_b[...] = jnp.zeros_like(acc_b)
    acc_c[...] = jnp.zeros_like(acc_c)
    def back_head(head):
        window, inside = head_window(head, head_dim)
        grad_head = gm_s[:, window] * inside
        probs = probs_s[head]
        grad_probs = nt_dot(grad_head, v_s[:, window])
        centre = jnp.sum(probs * grad_probs, axis=-1, keepdims=True)
        grad_scores = (probs * (grad_probs - centre) * scale).astype(low)
        acc_a[:, window] += nn_dot(grad_scores, k_s[:, window] * inside)
        acc_b[:, window] += tn_dot(grad_scores, q_s[:, window] * inside)
        acc_c[:, window] += tn_dot(probs.astype(low), grad_head)

    for head in range(HEADS // 2):
        back_head(head)

    wait_peers(mix_s, mix_r, mi_send, mi_recv, False)
    mixed_frames = unpack(frame_map, mix_r).astype(low)
    for j in range(2):
        term = tn_dot(mixed_frames, grads[:, j * att : (j + 1) * att])
        term = term.reshape(4, 4, share, att).astype(low)
        for level in range(4):
            for place in range(4):
                dwp[j, place, level] = term[level, place]
    pair_term = to_pair(dwp.at[1 - c], dw_in, pair_send.at[0], pair_recv.at[0])
    pair_term.start()

    for head in range(HEADS // 2, HEADS):
        back_head(head)

    def mate_copy(d):
        mate = lax.rem(plane + d, 4)
        return to_tm(dwa_s.at[mate], dwa_r.at[plane], da_send.at[mate], da_recv.at[plane], z * 4 + mate)

    pair_term.wait_recv()

    @pl.loop(0, 4)
    def _(place):
        both = dwp[c, place].astype(high) + dw_in[place].astype(high)
        dwa_s[place] = both.astype(low)

    for d in range(1, 4):
        mate_copy(d).start()
    dwa_r[plane] = dwa_s[plane]

    grad_rows = [acc[...].astype(low) for acc in (acc_a, acc_b, acc_c)]
    for j in range(2):
        shards = slice(j * SHARDS // 2, (j + 1) * SHARDS // 2)
        total = sum(
            nt_dot(grad_rows[i], wall[i, shards].reshape(SHARDS // 2 * depth, att)) for i in range(3)
        )
        pack(cell_map, total.astype(low), gn_s.at[j])
        send_peers(gn_s.at[j], gn_r.at[j], gn_send.at[pl.ds(j, 1)], gn_recv.at[pl.ds(j, 1)])

    for j in range(2):
        columns = slice(j * att, (j + 1) * att)
        update = nn_dot(mixed_frames, output_half(j))
        rows_out = tok[:, :, columns].reshape(count, att).astype(high) + update
        block_o[:, :, columns] = rows_out.astype(low).reshape(frames, cells, att)
    stores[0].start()
    scaled, inverse = norm_rows()

    def finish_items(h):
        pass_item(h, t, xn, 2).wait_send()
        pass_item(h, t, yn, 3).wait_send()
        for level in range(4):
            @pl.when((z < 3) & (level <= z))
            def _():
                pass_item(h, level * 4 + plane, xn, 0).wait_send()

            @pl.when((z > 0) & (level >= z))
            def _():
                pass_item(h, level * 4 + plane, xn, 1).wait_send()

            @pl.when(level != z)
            def _():
                pass_item(h, level * 4 + plane, xn, 2).wait_send()
                pass_item(h, level * 4 + plane, yn, 3).wait_send()
                pair_level(h, level * 4).wait_send()

            pass_item(h, level * 4 + plane, xn, 4).wait_send()
        for d in range(1, 4):
            pair_item(h, z * 4 + lax.rem(plane + d, 4)).wait_send()

    def level_copy(d):
        level = lax.rem(z + d, 4)
        return to_tm(dwb_s.at[level], dwb_r.at[z], db_send.at[level], db_recv.at[z], level * 4 + plane)

    for d in range(1, 4):
        mate = lax.rem(plane + d, 4)
        to_tm(dwa_s.at[mate], dwa_r.at[mate], da_send.at[mate], da_recv.at[mate], z * 4 + mate).wait_recv()
    dwb_s[...] = jnp.sum(dwa_r[...].astype(high), axis=0).astype(low)
    for d in range(1, 4):
        level_copy(d).start()
    dwb_r[z] = dwb_s[z]

    pair_term.wait_send()
    for h in range(2):
        finish_items(h)
    for d in range(1, 4):
        mate_copy(d).wait_send()
    wait_peers(gm_out, gm_in, gm_send, gm_recv, True)
    wait_peers(norm_s, norm_r, no_send, no_recv, True)
    wait_peers(mix_s, mix_r, mi_send, mi_recv, True)

    grad_parts = []
    for j in range(2):
        sems = (gn_send.at[pl.ds(j, 1)], gn_recv.at[pl.ds(j, 1)])
        wait_peers(gn_s.at[j], gn_r.at[j], *sems, False)
        grad_parts.append(unpack(frame_map, gn_r.at[j]))
    weighted = jnp.concatenate(grad_parts, axis=1) * gains
    first = jnp.mean(weighted, axis=-1, keepdims=True)
    second = jnp.mean(weighted * scaled, axis=-1, keepdims=True)
    result = inverse * (weighted - first - scaled * second)
    result = result + gout[...].reshape(count, width).astype(high)
    gtok_o[...] = result.astype(low).reshape(frames, cells, width)
    stores[1].start()

    for d in range(1, 4):
        level = lax.rem(z + d, 4)
        to_tm(dwb_s.at[level], dwb_r.at[level], db_send.at[level], db_recv.at[level], level * 4 + plane).wait_recv()
    dwf[c] = jnp.sum(dwb_r[...].astype(high), axis=0)
    pair_sum = to_pair(dwf.at[c], dwf.at[c], pair_send.at[1], pair_recv.at[1])
    pair_sum.start()

    to_pair(dwf.at[1 - c], dwf.at[1 - c], pair_send.at[1], pair_recv.at[1]).wait_recv()
    dw_o[:, :att] = dwf[0]
    dw_o[:, att:] = dwf[1]
    stores[2].start()

    pair_sum.wait_send()
    for d in range(1, 4):
        level_copy(d).wait_send()
    for j in range(2):
        sems = (gn_send.at[pl.ds(j, 1)], gn_recv.at[pl.ds(j, 1)])
        wait_peers(gn_s.at[j], gn_r.at[j], *sems, True)
    for store in stores:
        store.wait()


def on_chip_grid(
    frame_tokens,
    visible,
    grad_output,
    norm_gain,
    query_weight,
    key_weight,
    value_weight,
    output_weight,
):
    tokens = frame_tokens[0]
    frames, cells, width = tokens.shape
    groups = cells // SHARDS
    depth, att = query_weight.shape
    share = output_weight.shape[0]
    local = lax.dynamic_slice_in_dim(visible[0], lax.axis_index("tm") * groups, groups, 1)
    codes = local + 4 * jnp.arange(groups, dtype=jnp.int32)[None]
    rows, count = SHARDS * ROWS, frames * cells
    codes = jnp.pad(codes.reshape(1, count), ((0, 0), (0, rows - count)), constant_values=-1)
    low, high = jnp.bfloat16, jnp.float32
    vmem = pl.BlockSpec(memory_space=pltpu.VMEM)
    anywhere = pl.BlockSpec(memory_space=pl.ANY)
    like_tokens = pltpu.VMEM(tokens.shape, low)
    dma = pltpu.SemaphoreType.DMA
    wide = pltpu.VMEM((SHARDS, ROWS, width * 4 // 5), low)
    thin = pltpu.VMEM((SHARDS, ROWS, att * 4 // 5), low)
    two_thin = pltpu.VMEM((2, SHARDS, ROWS, att * 4 // 5), low)
    plain = pltpu.VMEM((count, att), low)
    total = pltpu.VMEM((count, att), high)
    quarter = pltpu.VMEM((4, 4, share, att), low)
    block_rows, grad_rows, grad_weight = pl.pallas_call(
        fused_kernel,
        out_shape=(
            jax.ShapeDtypeStruct(tokens.shape, low),
            jax.ShapeDtypeStruct(tokens.shape, low),
            jax.ShapeDtypeStruct((share, width), high),
        ),
        in_specs=[anywhere, anywhere, vmem, vmem, anywhere, anywhere, anywhere, anywhere],
        out_specs=(anywhere,) * 3,
        scratch_shapes=[
            like_tokens, like_tokens,
            pltpu.VMEM((share, width), low),
            like_tokens, like_tokens,
            pltpu.VMEM((share, width), high),
            pltpu.VMEM((4, SHARDS, depth, att), low),
            pltpu.VMEM((1 + frames, rows, count), low),
            pltpu.VMEM((1 + frames, rows, count), low),
            wide, wide,
            plain, plain, plain, plain,
            pltpu.VMEM((HEADS, count, count), high),
            total, total, total,
            thin, thin, thin, thin, two_thin, two_thin,
            pltpu.VMEM((2, 4, 4, share, att), low),
            quarter, quarter, quarter,
            pltpu.VMEM((4, share, att), low),
            pltpu.VMEM((4, share, att), low),
            pltpu.VMEM((2, share, att), high),
            dma((40,)),
            *[dma((2 * SHARDS,))] * 3,
            *[dma((1,))] * 6,
            *[dma((2,))] * 2,
            *[dma((4,))] * 4,
            dma((2,)),
            dma((2,)),
            dma((6,)),
            dma((3,)),
        ],
        compiler_params=pltpu.CompilerParams(
            collective_id=0, has_side_effects=True, vmem_limit_bytes=56 * 1024 * 1024
        ),
        name="temporal_block",
    )(
        tokens,
        grad_output[0],
        norm_gain,
        codes,
        query_weight,
        key_weight,
        value_weight,
        output_weight,
    )
    return (block_rows[None], grad_rows[None], grad_weight)


def solution(mesh):
    chip_grid = mesh.shape["tm"] == SHARDS and mesh.shape["dp"] == 2
    return jax.shard_map(
        on_chip_grid if chip_grid else on_device,
        mesh=mesh,
        in_specs=(
            P("dp", "tm", None, None),
            P("dp", None, None),
            P("dp", "tm", None, None),
            P(),
            P("tm", None),
            P("tm", None),
            P("tm", None),
            P("tm", None),
        ),
        out_specs=(P("dp", "tm", None, None), P("dp", "tm", None, None), P("tm", None)),
        check_vma=False,
    )
```
